256 devices in a mesh: row: 16 (over z_lo, y), col: 16 (over z_hi, x, core).
Axes of the slice: x: 4, y: 4, z: 8 (z_hi: 2, z_lo: 4; z = z_hi * 4 + z_lo), core: 2. Of those that a mesh axis runs over, the one named last changes fastest.
Arguments:
- tokens: bfloat16 [256, 256, 256], P('row', 'col'), may hold values from -6 to 6
- stale_kv: bfloat16 [256, 256, 512], P('row', 'col'), may hold values from -6 to 6
- timestep: int32 [1], replicated, may hold values from 0 to 999
- w_time: bfloat16 [256, 768], replicated, may hold values from -0.375 to 0.375
- w_qkv: bfloat16 [256, 768], replicated, may hold values from -20 to 20
- w_out: bfloat16 [256, 256], replicated, may hold values from -0.375 to 0.375
- w_merge: bfloat16 [1024, 768], replicated, may hold values from -0.1875 to 0.1875
- w_cqkv: bfloat16 [768, 1152], replicated, may hold values from -20 to 20
- w_cout: bfloat16 [384, 768], replicated, may hold values from -0.3125 to 0.3125
- w_up: bfloat16 [768, 1024], replicated, may hold values from -0.21875 to 0.21875
Outputs:
- fine_out: bfloat16 [256, 256, 256], P('row', 'col')
- fresh_kv: bfloat16 [256, 256, 512], P('row', 'col')
The draws below stay inside these ranges and needn't reach their ends.
All inputs are finite; a program needn't handle non-finite values.
Results may differ from the reference program's by a relative error of at most 0.034.
Values may be sent and summed in bfloat16 or wider, within the bound.
No kernel may reach another device: no remote copies, remote signals or barrier semaphores. Data moves between devices by JAX's collectives and lax.ppermute only.
A program may use at most 128 MiB of HBM per device.

```python
import math
import jax
import jax.numpy as jnp
from jax import lax

D = 256
DC = 768
HD = 64
CH = 6
TILE = 16
HEADS = 4
CW = 384
H = 256
W = 256
NC = 16384
N_ROW = 16
N_COL = 16


def projection_draw(key, rows, width, heads, head_size, low, high):
    first, second = jax.random.split(key)
    base = jnp.clip(jax.random.normal(first, (rows, 3 * width), jnp.float32), -3.0, 3.0) * rows ** (-0.5)
    strength = jax.random.permutation(second, jnp.linspace(low, high, heads, dtype=jnp.float32))
    columns = jnp.repeat(strength, head_size)
    query_part = base[:, :width] * columns[None, :]
    return jnp.concatenate([query_part, base[:, width:2 * width], base[:, 2 * width:]], axis=1).astype(jnp.bfloat16)


def draw_tokens(key, part):
    key = jax.random.fold_in(key, 11)
    first = jax.random.fold_in(key, 0)
    return jnp.clip(jax.random.normal(first, (H, W, D), jnp.float32), -6.0, 6.0).astype(jnp.bfloat16)


def draw_w_qkv(key, part):
    key = jax.random.fold_in(key, 12)
    return projection_draw(key, D, D, HEADS, HD, 6.0, 18.0)


def draw_w_cqkv(key, part):
    key = jax.random.fold_in(key, 13)
    return projection_draw(key, DC, CW, CH, HD, 6.0, 18.0)


def steps_of(key, dims, shards, smallest, top_value):
    level = 1.0
    for axis_at, blocks in shards:
        heights = jax.random.uniform(jax.random.fold_in(jax.random.fold_in(key, 6), axis_at), (blocks,), jnp.float32, smallest / len(shards), top_value / len(shards))
        level = level * jnp.repeat(jnp.exp(heights), dims[axis_at] // blocks).reshape((-1,) + (1,) * (len(dims) - 1 - axis_at))
    return level


def noise(own_key, dims, deviation, bound, cuts=(), kind=jnp.bfloat16):
    gain = steps_of(own_key, dims, cuts, -0.22, 0.18) if cuts else 1.0
    values = jax.random.normal(own_key, dims, jnp.float32) * deviation * gain
    return jnp.minimum(jnp.maximum(values, -bound), bound).astype(kind)


def setup_inputs(seed: int = 0) -> dict:
    key_of = jax.random.split(jax.random.key(seed), 11)
    tokens = draw_tokens(jax.random.fold_in(key_of[10], 71), 0)
    stale_kv = noise(key_of[1], (H, W, 2 * D), 1.0, 6.0, ((0, 16), (1, 16)))
    timestep = jax.random.randint(key_of[2], (1,), 0, 1000).astype(jnp.int32)
    w_time = noise(key_of[3], (D, 3 * D), D ** -0.5, 0.375)
    w_qkv = draw_w_qkv(jax.random.fold_in(key_of[10], 71), 0)
    w_out = noise(key_of[5], (D, D), D ** -0.5, 0.375)
    w_merge = noise(key_of[6], (4 * D, DC), (4 * D) ** -0.5, 0.1875)
    w_cqkv = draw_w_cqkv(jax.random.fold_in(key_of[10], 71), 0)
    w_cout = noise(key_of[8], (CW, DC), CW ** -0.5, 0.3125)
    w_up = noise(key_of[9], (DC, 4 * D), DC ** -0.5, 0.21875)
    return dict(tokens=tokens, stale_kv=stale_kv, timestep=timestep, w_time=w_time, w_qkv=w_qkv, w_out=w_out, w_merge=w_merge, w_cqkv=w_cqkv, w_cout=w_cout, w_up=w_up)


def layer_norm(values):
    values = values.astype(jnp.float32)
    mean = lax.optimization_barrier(jnp.mean(values, axis=-1, keepdims=True))
    centred = values - mean
    var = lax.optimization_barrier(jnp.mean(centred * centred, axis=-1, keepdims=True))
    return centred * lax.rsqrt(var + 1e-06)

def time_mod(timestep, w_time):
    half = w_time.shape[0] // 2
    freq = jnp.exp(-math.log(10000.0) * jnp.arange(half, dtype=jnp.float32) * 2.0 / w_time.shape[0])
    angle_t = timestep.astype(jnp.float32)[0] * freq
    emb = jnp.concatenate([jnp.cos(angle_t), jnp.sin(angle_t)])
    act = jax.nn.silu(emb).astype(jnp.bfloat16)
    return jnp.dot(act[None, :], w_time, preferred_element_type=jnp.float32)[0]

def neighbour_tile(query, kvpad, valid, heads, head_size):
    side = query.shape[0]
    width = query.shape[2]
    qf = query.reshape(side, side, heads, head_size).astype(jnp.float32)
    scores = []
    values = []
    for di in range(7):
        for dj in range(7):
            keys = kvpad[di:di + side, dj:dj + side, :width].reshape(side, side, heads, head_size).astype(jnp.float32)
            score = jnp.einsum('ijhd,ijhd->ijh', qf, keys) / math.sqrt(head_size)
            inside = valid[di:di + side, dj:dj + side][:, :, None] > 0.5
            scores.append(jnp.where(inside, score, -1e+30))
            values.append(kvpad[di:di + side, dj:dj + side, width:])
    scores = jnp.stack(scores)
    top = lax.optimization_barrier(jnp.max(scores, axis=0))
    expo = jnp.exp(scores - top[None])
    total = lax.optimization_barrier(jnp.sum(expo, axis=0))
    weights = expo.astype(jnp.bfloat16).astype(jnp.float32)
    acc = jnp.zeros((side, side, heads, head_size), jnp.float32)
    for index in range(49):
        vals = values[index].reshape(side, side, heads, head_size).astype(jnp.float32)
        acc = acc + weights[index][:, :, :, None] * vals
    return (acc / total[:, :, :, None]).reshape(side, side, width).astype(jnp.bfloat16)

def reference(tokens, stale_kv, timestep, w_time, w_qkv, w_out, w_merge, w_cqkv, w_cout, w_up):
    mod = time_mod(timestep, w_time)
    shift, scale, gate = (mod[:D], mod[D:2 * D], mod[2 * D:])
    normed = (layer_norm(tokens) * (1.0 + scale) + shift).astype(jnp.bfloat16)
    qkv = jnp.dot(normed.reshape(H * W, D), w_qkv, preferred_element_type=jnp.float32).astype(jnp.bfloat16).reshape(H, W, 3 * D)
    query = qkv[:, :, :D]
    fresh_kv = qkv[:, :, D:]
    stale_pad = jnp.pad(stale_kv, ((3, 3), (3, 3), (0, 0)))
    valid_pad = jnp.pad(jnp.ones((H, W), jnp.float32), ((3, 3), (3, 3)))

    def one_tile(number):
        number = number.astype(jnp.int32)
        row0 = number // N_COL * TILE
        col0 = number % N_COL * TILE
        zero = jnp.zeros((), jnp.int32)
        region = lax.dynamic_slice(stale_pad, (row0, col0, zero), (TILE + 6, TILE + 6, 2 * D))
        own = lax.dynamic_slice(fresh_kv, (row0, col0, zero), (TILE, TILE, 2 * D))
        region = lax.dynamic_update_slice(region, own, (jnp.int32(3), jnp.int32(3), zero))
        valid = lax.dynamic_slice(valid_pad, (row0, col0), (TILE + 6, TILE + 6))
        qtile = lax.dynamic_slice(query, (row0, col0, zero), (TILE, TILE, D))
        return neighbour_tile(qtile, region, valid, HEADS, HD)
    tiles = lax.map(one_tile, jnp.arange(N_ROW * N_COL, dtype=jnp.int32))
    attn = tiles.reshape(N_ROW, N_COL, TILE, TILE, D).transpose(0, 2, 1, 3, 4).reshape(H * W, D)
    mid = (tokens.reshape(H * W, D).astype(jnp.float32) + gate * jnp.dot(attn, w_out, preferred_element_type=jnp.float32)).astype(jnp.bfloat16)
    merged = mid.reshape(H // 2, 2, W // 2, 2, D).transpose(0, 2, 1, 3, 4).reshape(NC, 4 * D)
    coarse = jnp.dot(merged, w_merge, preferred_element_type=jnp.float32).astype(jnp.bfloat16)
    cnorm = layer_norm(coarse).astype(jnp.bfloat16)
    cqkv = jnp.dot(cnorm, w_cqkv, preferred_element_type=jnp.float32).astype(jnp.bfloat16)
    cq = cqkv[:, :CW].reshape(NC, CH, HD).transpose(1, 0, 2)
    ck = cqkv[:, CW:2 * CW].reshape(NC, CH, HD).transpose(1, 0, 2)
    cv = cqkv[:, 2 * CW:].reshape(NC, CH, HD).transpose(1, 0, 2)
    query_block = TILE * TILE // 4 * N_COL

    def one_head(parts):
        hq, hk, hv = parts

        def one_block(block_query):
            score = jnp.dot(block_query, hk.T, preferred_element_type=jnp.float32) / math.sqrt(HD)
            top = lax.optimization_barrier(jnp.max(score, axis=1, keepdims=True))
            expo = jnp.exp(score - top)
            total = lax.optimization_barrier(jnp.sum(expo, axis=1, keepdims=True))
            return jnp.dot(expo.astype(jnp.bfloat16), hv, preferred_element_type=jnp.float32) / total
        return lax.map(one_block, hq.reshape(NC // query_block, query_block, HD)).reshape(NC, HD)
    cattn = lax.map(one_head, (cq, ck, cv)).transpose(1, 0, 2).reshape(NC, CW).astype(jnp.bfloat16)
    coarse_mid = (coarse.astype(jnp.float32) + jnp.dot(cattn, w_cout, preferred_element_type=jnp.float32)).astype(jnp.bfloat16)
    upper = jnp.dot(coarse_mid, w_up, preferred_element_type=jnp.float32)
    upper = upper.reshape(H // 2, W // 2, 2, 2, D).transpose(0, 2, 1, 3, 4).reshape(H * W, D)
    fine_out = (mid.astype(jnp.float32) + upper).astype(jnp.bfloat16).reshape(H, W, D)
    return (fine_out, fresh_kv)
```

```python
import functools
import math

import jax
import jax.numpy as jnp
import numpy as np
from jax import lax
from jax.experimental import pallas as pl
from jax.experimental.pallas import tpu as pltpu
from jax.sharding import PartitionSpec as P

HD = 64
SIDE = 16
N = SIDE * SIDE
D = 256
BF = jnp.bfloat16
F32 = jnp.float32

PIECES = (
    (48, -3, 3, 0, 16),
    (48, 16, 3, 0, 16),
    (48, 0, 16, -3, 3),
    (48, 0, 16, 16, 3),
    (16, -3, 3, -3, 3),
    (16, -3, 3, 16, 3),
    (16, 16, 3, -3, 3),
    (16, 16, 3, 16, 3),
)
TOWARDS = ((1, 0), (-1, 0), (0, 1), (0, -1), (1, 1), (1, -1), (-1, 1), (-1, -1))


def halo_tables():
    pick = np.zeros((N, N), np.float32)
    place = np.full((8, 2 * N), -1000, np.int32)
    own = np.arange(N)
    place[0, :N] = own // SIDE
    place[1, :N] = own % SIDE
    at = 0
    for rows, i0, ni, j0, nj in PIECES:
        for number in range(ni * nj):
            i, j = i0 + number // nj, j0 + number % nj
            pick[at + number, (i % SIDE) * SIDE + j % SIDE] = 1.0
            place[0, N + at + number] = i
            place[1, N + at + number] = j
        at += rows
    return pick, place


def dot(a, b):
    return lax.dot_general(a, b, (((1,), (0,)), ((), ())), preferred_element_type=F32)


def dot_t(a, b):
    return lax.dot_general(a, b, (((1,), (1,)), ((), ())), preferred_element_type=F32)


def layer_norm(values):
    values = values.astype(F32)
    mean = jnp.mean(values, axis=-1, keepdims=True)
    centred = values - mean
    var = jnp.mean(centred * centred, axis=-1, keepdims=True)
    return centred * lax.rsqrt(var + 1e-06)


def natural_of(m):
    a, b, r, c = m >> 7, (m >> 6) & 1, (m >> 3) & 7, m & 7
    return (2 * r + a) * SIDE + 2 * c + b


def regroup_matrix():
    m = lax.broadcasted_iota(jnp.int32, (N, N), 0)
    n = lax.broadcasted_iota(jnp.int32, (N, N), 1)
    return (natural_of(m) == n).astype(F32).astype(BF)


def pack_kernel(pick_ref, stale_ref, *outs):
    at = 0
    for (rows, *_), out in zip(PIECES, outs):
        out[...] = dot(pick_ref[at : at + rows, :], stale_ref[...]).astype(BF)
        at += rows


def fine_project_kernel(time_ref, freq_ref, tokens_ref, w_time_ref, w_qkv_ref, q_ref, kv_ref, gate_ref, mine_ref):
    angle = time_ref[0].astype(F32) * freq_ref[...]
    emb = jnp.concatenate([jnp.cos(angle), jnp.sin(angle)], axis=1)
    act = (emb / (1.0 + jnp.exp(-emb))).astype(BF)
    mod = dot(jnp.broadcast_to(act, (16, D)), w_time_ref[...])[0:1, :]
    shift, scale, gate = mod[:, :D], mod[:, D : 2 * D], mod[:, 2 * D :]
    gate_ref[...] = jnp.broadcast_to(gate, (8, D))
    tokens = tokens_ref[...]
    normed = (layer_norm(tokens) * (1.0 + scale) + shift).astype(BF)
    kv_ref[...] = dot(normed, w_qkv_ref[:, D:]).astype(BF)
    regroup = regroup_matrix()
    q_ref[...] = dot(dot(regroup, normed).astype(BF), w_qkv_ref[:, :D]).astype(BF)
    mine_ref[...] = dot(regroup, tokens).astype(BF)


def fine_attend_kernel(place_ref, q_ref, kv_ref, gate_ref, mine_ref, *rest):
    pieces = rest[: len(PIECES)]
    w_out_ref, w_merge_ref, w_cqkv_ref, mid_ref, coarse_ref, cq_ref, ckv_ref, halo = rest[len(PIECES) :]
    at = 0
    for (rows, *_), piece in zip(PIECES, pieces):
        halo[at : at + rows, :] = piece[...]
        at += rows
    row0 = lax.axis_index("row") * SIDE
    col0 = lax.axis_index("col") * SIDE
    rows_all = lax.axis_size("row") * SIDE
    cols_all = lax.axis_size("col") * SIDE
    natural = natural_of(lax.broadcasted_iota(jnp.int32, (N, 1), 0))
    qi, qj = natural // SIDE, natural % SIDE
    ki, kj = place_ref[0:1, :], place_ref[1:2, :]
    in_image = (ki + row0 >= 0) & (ki + row0 < rows_all) & (kj + col0 >= 0) & (kj + col0 < cols_all)
    ki = jnp.where(in_image, ki, -1000)
    near = (jnp.abs(qi - ki) <= 3) & (jnp.abs(qj - kj) <= 3)
    lane = lax.broadcasted_iota(jnp.int32, (N, 128), 1)
    attn = []
    for pair in range(D // 128):
        cols = slice(pair * 128, pair * 128 + 128)
        vcols = slice(D + pair * 128, D + pair * 128 + 128)
        q2 = q_ref[:, cols]
        halves = []
        for which in range(2):
            q1 = jnp.where((lane < HD) if which == 0 else (lane >= HD), q2, jnp.zeros_like(q2))
            score = jnp.concatenate([dot_t(q1, kv_ref[:, cols]), dot_t(q1, halo[:, cols])], axis=1)
            score = jnp.where(near, score * (1.0 / math.sqrt(HD)), -1e30)
            expo = jnp.exp(score - jnp.max(score, axis=1, keepdims=True))
            total = jnp.sum(expo, axis=1, keepdims=True)
            weights = expo.astype(BF)
            acc = dot(weights[:, :N], kv_ref[:, vcols]) + dot(weights[:, N:], halo[:, vcols])
            halves.append(acc / total)
        attn.append(jnp.where(lane < HD, halves[0], halves[1]).astype(BF))
    attn = jnp.concatenate(attn, axis=1)
    mid = (mine_ref[...].astype(F32) + gate_ref[0:1, :] * dot(attn, w_out_ref[...])).astype(BF)
    mid_ref[...] = mid
    quarter = N // 4
    coarse = sum(
        dot(mid[part * quarter : (part + 1) * quarter, :], w_merge_ref[part * D : (part + 1) * D, :])
        for part in range(4)
    ).astype(BF)
    coarse_ref[...] = coarse
    cqkv = dot(layer_norm(coarse).astype(BF), w_cqkv_ref[...]).astype(BF)
    width = cq_ref.shape[1]
    cq_ref[...] = cqkv[:, :width]
    ckv_ref[...] = cqkv[:, width:]


def coarse_attend_kernel(q_ref, kv_ref, out_ref):
    width = q_ref.shape[1]
    block = 256
    lane = lax.broadcasted_iota(jnp.int32, (block, 128), 1)
    part, slot = lane >> 3, lane & 7
    ones = jnp.ones((kv_ref.shape[0], 128), BF)

    def step(number, unused):
        start = pl.multiple_of(number * block, block)
        stats = jnp.zeros((block, 128), F32)
        for pair in range(width // 128):
            cols = slice(pair * 128, pair * 128 + 128)
            q2 = q_ref[pl.ds(start, block), cols]
            values = jnp.concatenate([kv_ref[:, width + pair * 128 : width + pair * 128 + 128], ones], axis=1)
            halves = []
            for which in range(2):
                head = 2 * pair + which
                q1 = jnp.where((lane < HD) if which == 0 else (lane >= HD), q2, jnp.zeros_like(q2))
                score = dot_t(q1 * BF(1.0 / math.sqrt(HD)), kv_ref[:, cols])
                top = jnp.max(score, axis=1, keepdims=True)
                both = dot(jnp.exp(score - top).astype(BF), values)
                halves.append(both[:, :128])
                stats = jnp.where((slot == head) & (part < 3), top, stats)
                stats = jnp.where((slot == head) & (part >= 3) & (part < 5), both[:, 128:], stats)
            out_ref[pl.ds(start, block), cols] = jnp.where(lane < HD, halves[0], halves[1]).astype(BF)
        high = stats.astype(BF)
        rest = stats - high.astype(F32)
        middle = rest.astype(BF)
        low = (rest - middle.astype(F32)).astype(BF)
        first = (part == 0) | (part == 3)
        second = (part == 1) | (part == 4)
        out_ref[pl.ds(start, block), width:] = jnp.where(
            first, high.astype(F32), jnp.where(second, middle.astype(F32), low.astype(F32))
        ).astype(BF)
        return unused

    lax.fori_loop(0, q_ref.shape[0] // block, step, 0)


def finish_kernel(states_ref, coarse_ref, mid_ref, w_cout_ref, w_up_ref, out_ref):
    sources, count, _ = states_ref.shape
    width = w_cout_ref.shape[0]
    row = lax.broadcasted_iota(jnp.int32, (128, width), 0)
    head = lax.broadcasted_iota(jnp.int32, (128, width), 1) // HD
    part, slot = row >> 3, row & 7
    spread_top = ((slot == head) & (part < 3)).astype(F32).astype(BF)
    spread_total = ((slot == head) & (part >= 3) & (part < 5)).astype(F32).astype(BF)
    stats = states_ref[:, :, width:].reshape(sources * count, 128)
    tops = dot(stats, spread_top).reshape(sources, count, width)
    totals = dot(stats, spread_total).reshape(sources, count, width)
    best = jnp.max(tops, axis=0)
    factor = jnp.exp(tops - best[None])
    total = jnp.sum(totals * factor, axis=0)
    acc = jnp.sum(states_ref[:, :, :width].astype(F32) * factor, axis=0)
    cattn = (acc / total).astype(BF)
    coarse_mid = (coarse_ref[...].astype(F32) + dot(cattn, w_cout_ref[...])).astype(BF)
    upper = dot(coarse_mid, w_up_ref[...])
    upper = jnp.concatenate([upper[:, part * D : (part + 1) * D] for part in range(4)], axis=0)
    fine = (mid_ref[...].astype(F32) + upper).astype(BF)
    n = lax.broadcasted_iota(jnp.int32, (N, N), 0)
    m = lax.broadcasted_iota(jnp.int32, (N, N), 1)
    back = (natural_of(m) == n).astype(F32).astype(BF)
    out_ref[...] = dot(back, fine).astype(BF)


def call(kernel, outs, scratch=(), smem=0):
    vmem = pl.BlockSpec(memory_space=pltpu.VMEM)

    def run(*args):
        return pl.pallas_call(
            kernel,
            out_shape=[jax.ShapeDtypeStruct(shape, kind) for shape, kind in outs],
            in_specs=[pl.BlockSpec(memory_space=pltpu.SMEM)] * smem + [vmem] * (len(args) - smem),
            out_specs=[vmem] * len(outs),
            scratch_shapes=list(scratch),
            compiler_params=pltpu.CompilerParams(vmem_limit_bytes=48 * 1024 * 1024),
        )(*args)

    return run


def shifted(piece, down, right):
    rows, cols = lax.axis_size("row"), lax.axis_size("col")
    pairs = [
        (i * cols + j, (i + down) * cols + j + right)
        for i in range(rows)
        for j in range(cols)
        if 0 <= i + down < rows and 0 <= j + right < cols
    ]
    return lax.ppermute(piece, ("row", "col"), pairs)


def gathered_rows(block):
    size = lax.axis_size("row")
    for step in (4, 1):
        def to(i, k):
            if step == 4:
                return (i + 4 * k) % size
            return i // 4 * 4 + (i + k) % 4

        parts = [block] + [lax.ppermute(block, "row", [(i, to(i, k)) for i in range(size)]) for k in (1, 2, 3)]
        block = jnp.concatenate(parts, axis=0)
    return block


def per_device(tokens, stale_kv, timestep, w_time, w_qkv, w_out, w_merge, w_cqkv, w_cout, w_up):
    width = w_cout.shape[0]
    coarse_width = w_cout.shape[1]
    count = N // 4
    pick, place = halo_tables()
    pieces = call(pack_kernel, [((rows, 2 * D), BF) for rows, *_ in PIECES])(
        jnp.asarray(pick, BF), stale_kv.reshape(N, 2 * D)
    )
    pieces = [shifted(piece, *towards) for piece, towards in zip(pieces, TOWARDS)]
    freq = np.exp(-math.log(10000.0) * np.arange(D // 2, dtype=np.float32) * 2.0 / D).astype(np.float32)[None]
    query, fresh_kv, gate, mine = call(
        fine_project_kernel, [((N, D), BF), ((N, 2 * D), BF), ((8, D), F32), ((N, D), BF)], smem=1
    )(timestep, jnp.asarray(freq), tokens.reshape(N, D), w_time, w_qkv)
    mid, coarse, cquery, ckv = call(
        fine_attend_kernel,
        [((N, D), BF), ((count, coarse_width), BF), ((count, width), BF), ((count, 2 * width), BF)],
        scratch=[pltpu.VMEM((N, 2 * D), BF)],
    )(jnp.asarray(place), query, fresh_kv, gate, mine, *pieces, w_out, w_merge, w_cqkv)
    strip = lax.all_gather(cquery, "col", axis=0, tiled=True)
    keys_values = gathered_rows(ckv)
    (states,) = call(coarse_attend_kernel, [((strip.shape[0], width + 128), BF)])(strip, keys_values)
    states = lax.all_to_all(states.reshape(lax.axis_size("col"), count, width + 128), "col", 0, 0)
    (fine_out,) = call(finish_kernel, [((N, D), BF)])(states, coarse, mid, w_cout, w_up)
    return (fine_out.reshape(SIDE, SIDE, D), fresh_kv.reshape(SIDE, SIDE, 2 * D))


def solution(mesh):
    placed = (P("row", "col", None), P("row", "col", None), P(), P(), P(), P(), P(), P(), P(), P())
    return jax.shard_map(
        per_device,
        mesh=mesh,
        in_specs=placed,
        out_specs=(P("row", "col", None), P("row", "col", None)),
        check_vma=False,
    )
```

```python
import itertools
import math

import jax
import jax.numpy as jnp
import numpy as np
from jax import lax
from jax.experimental import pallas as pl
from jax.experimental.pallas import tpu as pltpu
from jax.sharding import Mesh
from jax.sharding import PartitionSpec as P

HD = 64
SIDE = 16
N = SIDE * SIDE
D = 256
BAND = 3 * SIDE
EDGE = 80
BF = jnp.bfloat16
F32 = jnp.float32
AXES = ("zl", "y", "zh", "x", "core")
SIZES = (4, 4, 2, 4, 2)


def dot(a, b):
    return lax.dot_general(a, b, (((1,), (0,)), ((), ())), preferred_element_type=F32)


def dot_t(a, b):
    return lax.dot_general(a, b, (((1,), (1,)), ((), ())), preferred_element_type=F32)


def one_hot(condition):
    return condition.astype(F32).astype(BF)


def iota(shape, dim):
    return lax.broadcasted_iota(jnp.int32, shape, dim)


def tile_row():
    return lax.axis_index("zl") * 4 + lax.axis_index("y")


def tile_col():
    return lax.axis_index("zh") * 8 + lax.axis_index("x") * 2 + lax.axis_index("core")


def third(n):
    return (n * 171) >> 9


def layer_norm(values):
    values = values.astype(F32)
    mean = jnp.mean(values, axis=-1, keepdims=True)
    centred = values - mean
    var = jnp.mean(centred * centred, axis=-1, keepdims=True)
    return centred * lax.rsqrt(var + 1e-06)


def natural_of(m):
    a, b, r, c = m >> 7, (m >> 6) & 1, (m >> 3) & 7, m & 7
    return (2 * r + a) * SIDE + 2 * c + b


def rows_kernel(stale_ref, near_ref, far_ref, all_ref, sems):
    odd = tile_row() % 2
    last = 13
    copies = [
        pltpu.make_async_copy(stale_ref.at[pl.ds((1 - odd) * last, 3)], near_ref, sems.at[0]),
        pltpu.make_async_copy(stale_ref.at[pl.ds(odd * last, 3)], far_ref, sems.at[1]),
        pltpu.make_async_copy(stale_ref, all_ref, sems.at[2]),
    ]
    for copy in copies:
        copy.start()
    for copy in copies:
        copy.wait()


def columns_kernel(stale_ref, row_near_ref, row_far_ref, near_ref, far_ref):
    odd = tile_col() % 2
    stale = stale_ref[...].reshape(N, 2 * D)
    row_near = row_near_ref[...].reshape(BAND, 2 * D)
    row_far = row_far_ref[...].reshape(BAND, 2 * D)
    for out, first in ((near_ref, (1 - odd) * 13), (far_ref, odd * 13)):
        take, source = iota((BAND, N), 0), iota((BAND, N), 1)
        i = third(take)
        out[:BAND, :] = dot(one_hot(source == i * SIDE + first + take - 3 * i), stale).astype(BF)
        take, source = iota((SIDE, BAND), 0), iota((SIDE, BAND), 1)
        i = third(take)
        corner = one_hot((source == i * SIDE + first + take - 3 * i) & (take < 9))
        out[BAND : BAND + SIDE, :] = dot(corner, row_near).astype(BF)
        out[BAND + SIDE :, :] = dot(corner, row_far).astype(BF)


def project_kernel(time_ref, tokens_hbm, w_time_hbm, w_qkv_hbm, w_out_hbm, w_merge_hbm, w_cqkv_hbm,
                   q_ref, kv_ref, kv_out_ref, gate_ref, mine_ref, w_out_ref, w_merge_ref, w_cqkv_ref,
                   tokens_ref, w_time_ref, w_qkv_ref, sems):
    pairs = (
        (tokens_hbm, tokens_ref),
        (w_time_hbm, w_time_ref),
        (w_qkv_hbm, w_qkv_ref),
        (w_out_hbm, w_out_ref),
        (w_merge_hbm, w_merge_ref),
        (w_cqkv_hbm, w_cqkv_ref),
    )
    copies = [pltpu.make_async_copy(a, b, sems.at[k]) for k, (a, b) in enumerate(pairs)]
    for copy in copies:
        copy.start()
    half = D // 2
    index = iota((8, half), 1).astype(F32)
    angle = time_ref[0].astype(F32) * jnp.exp(-math.log(10000.0) * index * 2.0 / D)
    emb = jnp.concatenate([jnp.cos(angle), jnp.sin(angle)], axis=1)
    act = (emb / (1.0 + jnp.exp(-emb))).astype(BF)
    regroup = one_hot(natural_of(iota((N, N), 0)) == iota((N, N), 1))
    copies[0].wait()
    tokens = tokens_ref[...]
    mine_ref[...] = dot(regroup, tokens).astype(BF)
    normal = layer_norm(tokens)
    copies[1].wait()
    mod = dot(act, w_time_ref[...])
    gate_ref[...] = mod[:, 2 * D :]
    normed = (normal * (1.0 + mod[0:1, D : 2 * D]) + mod[0:1, :D]).astype(BF)
    copies[2].wait()
    kv = dot(normed, w_qkv_ref[:, D:]).astype(BF)
    kv_ref[...] = kv
    kv_out_ref[...] = kv
    q_ref[...] = dot(dot(regroup, normed).astype(BF), w_qkv_ref[:, :D]).astype(BF)
    for copy in copies[3:]:
        copy.wait()


def fine_kernel(q_ref, kv_ref, gate_ref, mine_ref, row_near_ref, row_far_ref, col_near_ref, col_far_ref,
                w_out_ref, w_merge_ref, w_cqkv_ref,
                mid_ref, coarse_ref, cq_ref, ckv_ref, other_ref, halo):
    halo[:BAND, :] = row_near_ref[...].reshape(BAND, 2 * D)
    halo[BAND : 2 * BAND, :] = row_far_ref[...].reshape(BAND, 2 * D)
    halo[2 * BAND : 2 * BAND + EDGE, :] = col_near_ref[...]
    halo[2 * BAND + EDGE :, :] = col_far_ref[...]

    row, col = tile_row(), tile_col()
    row_odd, col_odd = row % 2, col % 2

    def after(odd):
        return (1 - odd) * SIDE - 3 * odd

    near_i, far_i = after(row_odd), after(1 - row_odd)
    near_j, far_j = after(col_odd), after(1 - col_odd)
    k = iota((1, N), 1)
    own_i, own_j = k >> 4, k & 15
    edge = jnp.where(k >= 2 * BAND + EDGE, k - 2 * BAND - EDGE, k - 2 * BAND)
    edge = jnp.maximum(edge, 0)
    cut = jnp.where(edge < BAND, edge, (edge - BAND) & 15)
    step = third(cut)
    side_i = jnp.where(edge < BAND, step, jnp.where(edge < BAND + SIDE, near_i, far_i) + step)
    side_j = jnp.where(k >= 2 * BAND + EDGE, far_j, near_j) + cut - 3 * step
    side_i = jnp.where((edge >= BAND) & (cut >= 9), -1000, side_i)
    band = jnp.where(k >= BAND, k - BAND, k)
    band_i = jnp.where(k >= BAND, far_i, near_i) + (band >> 4)
    halo_i = jnp.where(k < 2 * BAND, band_i, side_i)
    halo_j = jnp.where(k < 2 * BAND, band & 15, side_j)
    ki = jnp.concatenate([own_i, halo_i], axis=1)
    kj = jnp.concatenate([own_j, halo_j], axis=1)
    at_i, at_j = ki + row * SIDE, kj + col * SIDE
    in_image = (at_i >= 0) & (at_i < 16 * SIDE) & (at_j >= 0) & (at_j < 16 * SIDE)
    ki = jnp.where(in_image, ki, -1000)
    natural = natural_of(iota((N, 1), 0))
    near = (jnp.abs((natural >> 4) - ki) <= 3) & (jnp.abs((natural & 15) - kj) <= 3)

    lane = iota((N, 128), 1)
    attn = []
    for pair in range(D // 128):
        cols = slice(pair * 128, pair * 128 + 128)
        vcols = slice(D + pair * 128, D + pair * 128 + 128)
        q2 = q_ref[:, cols]
        halves = []
        for which in range(2):
            q1 = jnp.where((lane < HD) if which == 0 else (lane >= HD), q2, jnp.zeros_like(q2))
            score = jnp.concatenate([dot_t(q1, kv_ref[:, cols]), dot_t(q1, halo[:, cols])], axis=1)
            score = jnp.where(near, score * (1.0 / math.sqrt(HD)), -1e30)
            expo = jnp.exp(score - jnp.max(score, axis=1, keepdims=True))
            total = jnp.sum(expo, axis=1, keepdims=True)
            weights = expo.astype(BF)
            acc = dot(weights[:, :N], kv_ref[:, vcols]) + dot(weights[:, N:], halo[:, vcols])
            halves.append(acc / total)
        attn.append(jnp.where(lane < HD, halves[0], halves[1]).astype(BF))
    attn = jnp.concatenate(attn, axis=1)
    mid = (mine_ref[...].astype(F32) + gate_ref[0:1, :] * dot(attn, w_out_ref[...])).astype(BF)
    mid_ref[...] = mid
    quarter = N // 4
    coarse = sum(
        dot(mid[part * quarter : (part + 1) * quarter, :], w_merge_ref[part * D : (part + 1) * D, :])
        for part in range(4)
    ).astype(BF)
    coarse_ref[...] = coarse
    cqkv = dot(layer_norm(coarse).astype(BF), w_cqkv_ref[...]).astype(BF)
    width = w_cqkv_ref.shape[1] // 3
    half = width // 2
    halves = []
    for which in range(2):
        starts = [part * width + which * half for part in range(3)]
        halves.append([cqkv[:, start : start + half] for start in starts])
    core = lax.axis_index("core")
    mine = [jnp.where(core == 0, a, b) for a, b in zip(*halves)]
    theirs = [jnp.where(core == 0, b, a) for a, b in zip(*halves)]
    cq_ref[...] = mine[0]
    ckv_ref[...] = jnp.concatenate(mine[1:], axis=1)
    other_ref[...] = jnp.concatenate(theirs, axis=1)


def chip_kernel(cq_ref, ckv_ref, other_ref, q_ref, kv_ref):
    count, half = cq_ref.shape
    for chip in range(q_ref.shape[0]):
        q_ref[chip, :count, :] = cq_ref[...]
        q_ref[chip, count:, :] = other_ref[:, :half]
    kv_ref[:count, :] = ckv_ref[...]
    kv_ref[count:, :] = other_ref[:, half:]


def coarse_kernel(q_ref, *rest):
    pieces, out_ref = rest[:-1], rest[-1]
    block = q_ref.shape[1]
    lane = iota((block, 128), 1)
    low = lane < HD
    part, slot = lane >> 3, lane & 7
    kv = jnp.concatenate([piece[...] for piece in pieces], axis=0)
    ones = jnp.ones((kv.shape[0], 128), BF)
    values = [jnp.concatenate([kv[:, cols : cols + 128], ones], axis=1) for cols in (128, 256)]
    scale = BF(1.0 / math.sqrt(HD))

    def step(number, unused):
        q2 = q_ref[number, :, :128] * scale
        q3 = q_ref[number, :, 128:] * scale
        zero = jnp.zeros_like(q2)
        scores = [
            dot_t(jnp.where(low, q2, zero), kv[:, :128]),
            dot_t(jnp.where(low, zero, q2), kv[:, :128]),
            dot_t(q3, kv[:, 128:192]),
        ]
        stats = jnp.zeros((block, 128), F32)
        accs = []
        for head, score in enumerate(scores):
            top = jnp.max(score, axis=1, keepdims=True)
            both = dot(jnp.exp(score - top).astype(BF), values[0 if head == 0 else 1])
            accs.append(both[:, :128])
            stats = jnp.where((slot == head) & (part < 3), top, stats)
            stats = jnp.where((slot == head) & (part >= 3), both[:, 128:], stats)
        high = stats.astype(BF).astype(F32)
        middle = (stats - high).astype(BF).astype(F32)
        last = stats - high - middle
        stats = jnp.where((part == 0) | (part == 3), high, jnp.where((part == 1) | (part == 4), middle, last))
        out_ref[number, :, :128] = jnp.where(low, accs[1], accs[2]).astype(BF)
        out_ref[number, :, 128:] = jnp.where(low, stats, accs[0]).astype(BF)
        return unused

    lax.fori_loop(0, q_ref.shape[0], step, 0)


def merge_kernel(states_ref, mine_ref, other_ref):
    sources, count, _ = states_ref.shape
    row, column = iota((128, 256), 0), iota((128, 256), 1)
    head = jnp.where(column < HD, 1, jnp.where(column < 2 * HD, 2, 0))
    part, slot = row >> 3, row & 7
    stats = states_ref[:, :, 128:].reshape(sources * count, 128)
    tops = dot(stats, one_hot((slot == head) & (part < 3))).reshape(sources, count, 256)
    totals = dot(stats, one_hot((slot == head) & (part >= 3) & (part < 5))).reshape(sources, count, 256)
    factor = jnp.exp(tops - jnp.max(tops, axis=0)[None])
    total = jnp.sum(totals * factor, axis=0)
    acc = jnp.sum(states_ref[...].astype(F32) * factor, axis=0)
    cattn = (acc / total).astype(BF)
    cattn = jnp.concatenate([cattn[:, 3 * HD :], cattn[:, : 2 * HD]], axis=1)
    mine_ref[...] = cattn[: count // 2]
    other_ref[...] = cattn[count // 2 :]


def finish_kernel(mine_ref, other_ref, coarse_ref, mid_ref, w_cout_ref, w_up_ref, out_ref):
    half = mine_ref.shape[1]
    core = lax.axis_index("core")
    attended = dot(mine_ref[...], w_cout_ref[pl.ds(pl.multiple_of(core * half, half), half), :])
    attended += dot(other_ref[...], w_cout_ref[pl.ds(pl.multiple_of((1 - core) * half, half), half), :])
    coarse_mid = (coarse_ref[...].astype(F32) + attended).astype(BF)
    upper = dot(coarse_mid, w_up_ref[...])
    upper = jnp.concatenate([upper[:, part * D : (part + 1) * D] for part in range(4)], axis=0)
    fine = (mid_ref[...].astype(F32) + upper).astype(BF)
    out_ref[...] = dot(one_hot(natural_of(iota((N, N), 1)) == iota((N, N), 0)), fine).astype(BF)


def call(kernel, outs, spaces=None, scratch=()):
    vmem = pl.BlockSpec(memory_space=pltpu.VMEM)

    def run(*args):
        given = spaces or [pltpu.VMEM] * len(args)
        return pl.pallas_call(
            kernel,
            out_shape=[jax.ShapeDtypeStruct(shape, BF if kind is None else kind) for shape, kind in outs],
            in_specs=[pl.BlockSpec(memory_space=space) for space in given],
            out_specs=[vmem] * len(outs),
            scratch_shapes=list(scratch),
            compiler_params=pltpu.CompilerParams(vmem_limit_bytes=48 * 1024 * 1024),
        )(*args)

    return run


def permuted(value, target):
    pairs = []
    for at in itertools.product(*(range(size) for size in SIZES)):
        to = target(*at)
        if to is not None:
            pairs.append((int(np.ravel_multi_index(at, SIZES)), int(np.ravel_multi_index(to, SIZES))))
    return lax.ppermute(value, AXES, pairs)


def partner(index, far):
    other = index ^ 1 if not far else (index + 1 if index % 2 else index - 1)
    return other if 0 <= other < 16 else None


def row_partner(far):
    def target(zl, y, zh, x, core):
        to = partner(zl * 4 + y, far)
        return None if to is None else (to // 4, to % 4, zh, x, core)

    return target


def col_partner(far):
    def target(zl, y, zh, x, core):
        to = partner(zh * 8 + x * 2 + core, far)
        return None if to is None else (zl, y, to // 8, to // 2 % 4, to % 2)

    return target


def along_z(step):
    def target(zl, y, zh, x, core):
        z = (zh * 4 + zl + step) % 8
        return (z % 4, y, z // 4, x, core)

    return target


def other_core(zl, y, zh, x, core):
    return (zl, y, zh, x, 1 - core)


def per_device(tokens, stale_kv, timestep, w_time, w_qkv, w_out, w_merge, w_cqkv, w_cout, w_up):
    width, coarse_width = w_cout.shape
    half = width // 2
    count = N // 4
    hbm, vmem = pl.ANY, pltpu.VMEM
    band = ((3, SIDE, 2 * D), None)
    row_near, row_far, stale = call(
        rows_kernel, [band, band, (stale_kv.shape, None)], [hbm], [pltpu.SemaphoreType.DMA((3,))]
    )(stale_kv)
    row_near = permuted(row_near, row_partner(False))
    row_far = permuted(row_far, row_partner(True))
    query, kv, fresh_kv, gate, mine, w_out, w_merge, w_cqkv = call(
        project_kernel,
        [((N, D), None), ((N, 2 * D), None), ((N, 2 * D), None), ((8, D), F32), ((N, D), None)]
        + [(w.shape, None) for w in (w_out, w_merge, w_cqkv)],
        [pltpu.SMEM] + [hbm] * 6,
        [pltpu.VMEM((N, D), BF), pltpu.VMEM(w_time.shape, BF), pltpu.VMEM(w_qkv.shape, BF), pltpu.SemaphoreType.DMA((6,))],
    )(timestep, tokens.reshape(N, D), w_time, w_qkv, w_out, w_merge, w_cqkv)
    col_near, col_far = call(columns_kernel, [((EDGE, 2 * D), None)] * 2)(stale, row_near, row_far)
    col_near = permuted(col_near, col_partner(False))
    col_far = permuted(col_far, col_partner(True))
    mid, coarse, cq, ckv, other = call(
        fine_kernel,
        [((N, D), None), ((count, coarse_width), None), ((count, half), None), ((count, width), None), ((count, 3 * half), None)],
        scratch=[pltpu.VMEM((N, 2 * D), BF)],
    )(query, kv, gate, mine, row_near, row_far, col_near, col_far, w_out, w_merge, w_cqkv)
    other = permuted(other, other_core)
    queries, block = call(chip_kernel, [((16, 2 * count, half), None), ((2 * count, width), None)])(cq, ckv, other)
    up = down = block
    blocks = [block]
    for _ in range(3):
        up, down = permuted(up, along_z(1)), permuted(down, along_z(-1))
        blocks += [up, down]
    blocks += [permuted(up[:count], along_z(1)), permuted(down[count:], along_z(-1))]
    queries = lax.all_to_all(queries, ("y", "x"), 0, 0)
    (states,) = call(coarse_kernel, [((16, 2 * count, 256), None)])(queries, *blocks)
    states = lax.all_to_all(states, ("y", "x"), 0, 0)
    attn, other = call(merge_kernel, [((count, half), None)] * 2)(states)
    other = permuted(other, other_core)
    (fine_out,) = call(finish_kernel, [((N, D), None)])(attn, other, coarse, mid, w_cout, w_up)
    return (fine_out.reshape(SIDE, SIDE, D), fresh_kv.reshape(SIDE, SIDE, 2 * D))


def solution(mesh):
    fine = Mesh(mesh.devices.reshape(SIZES), AXES)
    tiled = P(("zl", "y"), ("zh", "x", "core"), None)
    return jax.shard_map(
        per_device,
        mesh=fine,
        in_specs=(tiled, tiled) + (P(),) * 8,
        out_specs=(tiled, tiled),
        check_vma=False,
    )
```

```python
import functools
import itertools
import math

import jax
import jax.numpy as jnp
import numpy as np
from jax import lax
from jax.experimental import pallas as pl
from jax.experimental.pallas import tpu as pltpu
from jax.sharding import Mesh
from jax.sharding import PartitionSpec as P

HD = 64
SIDE = 16
N = SIDE * SIDE
D = 256
BAND = 3 * SIDE
EDGE = 80
BF = jnp.bfloat16
F32 = jnp.float32
AXES = ("zl", "y", "zh", "x", "core")
SIZES = (4, 4, 2, 4, 2)


def dot(a, b):
    return lax.dot_general(a, b, (((1,), (0,)), ((), ())), preferred_element_type=F32)


def dot_t(a, b):
    return lax.dot_general(a, b, (((1,), (1,)), ((), ())), preferred_element_type=F32)


def one_hot(condition):
    return condition.astype(F32).astype(BF)


def iota(shape, dim):
    return lax.broadcasted_iota(jnp.int32, shape, dim)


def tile_row():
    return lax.axis_index("zl") * 4 + lax.axis_index("y")


def tile_col():
    return lax.axis_index("zh") * 8 + lax.axis_index("x") * 2 + lax.axis_index("core")


def third(n):
    return (n * 171) >> 9


def layer_norm(values):
    values = values.astype(F32)
    mean = jnp.mean(values, axis=-1, keepdims=True)
    centred = values - mean
    var = jnp.mean(centred * centred, axis=-1, keepdims=True)
    return centred * lax.rsqrt(var + 1e-06)


def natural_of(m):
    a, b, r, c = m >> 7, (m >> 6) & 1, (m >> 3) & 7, m & 7
    return (2 * r + a) * SIDE + 2 * c + b


def rows_kernel(stale_ref, near_ref, far_ref):
    odd = tile_row() % 2
    near_ref[...] = stale_ref[pl.ds((1 - odd) * 13, 3)]
    far_ref[...] = stale_ref[pl.ds(odd * 13, 3)]


def columns_kernel(stale_ref, row_near_ref, row_far_ref, near_ref, far_ref):
    odd = tile_col() % 2
    stale = stale_ref[...].reshape(N, 2 * D)
    row_near = row_near_ref[...].reshape(BAND, 2 * D)
    row_far = row_far_ref[...].reshape(BAND, 2 * D)
    for out, first in ((near_ref, (1 - odd) * 13), (far_ref, odd * 13)):
        take, source = iota((BAND, N), 0), iota((BAND, N), 1)
        i = third(take)
        out[:BAND, :] = dot(one_hot(source == i * SIDE + first + take - 3 * i), stale).astype(BF)
        take, source = iota((SIDE, BAND), 0), iota((SIDE, BAND), 1)
        i = third(take)
        corner = one_hot((source == i * SIDE + first + take - 3 * i) & (take < 9))
        out[BAND : BAND + SIDE, :] = dot(corner, row_near).astype(BF)
        out[BAND + SIDE :, :] = dot(corner, row_far).astype(BF)


def project_kernel(time_ref, tokens_ref, w_time_ref, w_qkv_ref, q_ref, kv_ref, kv_out_ref, gate_ref, mine_ref):
    half = D // 2
    index = iota((8, half), 1).astype(F32)
    angle = time_ref[0].astype(F32) * jnp.exp(-math.log(10000.0) * index * 2.0 / D)
    emb = jnp.concatenate([jnp.cos(angle), jnp.sin(angle)], axis=1)
    act = (emb / (1.0 + jnp.exp(-emb))).astype(BF)
    mod = dot(act, w_time_ref[...])
    gate_ref[...] = mod[:, 2 * D :]
    regroup = one_hot(natural_of(iota((N, N), 0)) == iota((N, N), 1))
    tokens = tokens_ref[...]
    mine_ref[...] = dot(regroup, tokens).astype(BF)
    normed = (layer_norm(tokens) * (1.0 + mod[0:1, D : 2 * D]) + mod[0:1, :D]).astype(BF)
    kv = dot(normed, w_qkv_ref[:, D:]).astype(BF)
    kv_ref[...] = kv
    kv_out_ref[...] = kv
    q_ref[...] = dot(dot(regroup, normed).astype(BF), w_qkv_ref[:, :D]).astype(BF)


def fine_kernel(q_ref, kv_ref, gate_ref, mine_ref, row_near_ref, row_far_ref, col_near_ref, col_far_ref,
                w_out_ref, w_merge_ref, w_cqkv_ref,
                mid_ref, coarse_ref, mine_out_ref, other_ref, ckv_ref, halo):
    halo[:BAND, :] = row_near_ref[...].reshape(BAND, 2 * D)
    halo[BAND : 2 * BAND, :] = row_far_ref[...].reshape(BAND, 2 * D)
    halo[2 * BAND : 2 * BAND + EDGE, :] = col_near_ref[...]
    halo[2 * BAND + EDGE :, :] = col_far_ref[...]

    row, col = tile_row(), tile_col()
    row_odd, col_odd = row % 2, col % 2

    def after(odd):
        return (1 - odd) * SIDE - 3 * odd

    near_i, far_i = after(row_odd), after(1 - row_odd)
    near_j, far_j = after(col_odd), after(1 - col_odd)
    k = iota((1, N), 1)
    own_i, own_j = k >> 4, k & 15
    edge = jnp.where(k >= 2 * BAND + EDGE, k - 2 * BAND - EDGE, k - 2 * BAND)
    edge = jnp.maximum(edge, 0)
    cut = jnp.where(edge < BAND, edge, (edge - BAND) & 15)
    step = third(cut)
    side_i = jnp.where(edge < BAND, step, jnp.where(edge < BAND + SIDE, near_i, far_i) + step)
    side_j = jnp.where(k >= 2 * BAND + EDGE, far_j, near_j) + cut - 3 * step
    side_i = jnp.where((edge >= BAND) & (cut >= 9), -1000, side_i)
    band = jnp.where(k >= BAND, k - BAND, k)
    band_i = jnp.where(k >= BAND, far_i, near_i) + (band >> 4)
    halo_i = jnp.where(k < 2 * BAND, band_i, side_i)
    halo_j = jnp.where(k < 2 * BAND, band & 15, side_j)
    ki = jnp.concatenate([own_i, halo_i], axis=1)
    kj = jnp.concatenate([own_j, halo_j], axis=1)
    at_i, at_j = ki + row * SIDE, kj + col * SIDE
    in_image = (at_i >= 0) & (at_i < 16 * SIDE) & (at_j >= 0) & (at_j < 16 * SIDE)
    ki = jnp.where(in_image, ki, -1000)
    natural = natural_of(iota((N, 1), 0))
    near = (jnp.abs((natural >> 4) - ki) <= 3) & (jnp.abs((natural & 15) - kj) <= 3)

    lane = iota((N, 128), 1)
    attn = []
    for pair in range(D // 128):
        cols = slice(pair * 128, pair * 128 + 128)
        vcols = slice(D + pair * 128, D + pair * 128 + 128)
        q2 = q_ref[:, cols]
        halves = []
        for which in range(2):
            q1 = jnp.where((lane < HD) if which == 0 else (lane >= HD), q2, jnp.zeros_like(q2))
            score = jnp.concatenate([dot_t(q1, kv_ref[:, cols]), dot_t(q1, halo[:, cols])], axis=1)
            score = jnp.where(near, score * (1.0 / math.sqrt(HD)), -1e30)
            expo = jnp.exp(score - jnp.max(score, axis=1, keepdims=True))
            total = jnp.sum(expo, axis=1, keepdims=True)
            weights = expo.astype(BF)
            acc = dot(weights[:, :N], kv_ref[:, vcols]) + dot(weights[:, N:], halo[:, vcols])
            halves.append(acc / total)
        attn.append(jnp.where(lane < HD, halves[0], halves[1]).astype(BF))
    attn = jnp.concatenate(attn, axis=1)
    mid = (mine_ref[...].astype(F32) + gate_ref[0:1, :] * dot(attn, w_out_ref[...])).astype(BF)
    mid_ref[...] = mid
    quarter = N // 4
    coarse = sum(
        dot(mid[part * quarter : (part + 1) * quarter, :], w_merge_ref[part * D : (part + 1) * D, :])
        for part in range(4)
    ).astype(BF)
    coarse_ref[...] = coarse
    cqkv = dot(layer_norm(coarse).astype(BF), w_cqkv_ref[...]).astype(BF)
    width = w_cqkv_ref.shape[1] // 3
    half = width // 2
    halves = []
    for which in range(2):
        starts = [part * width + which * half for part in range(3)]
        halves.append([cqkv[:, start : start + half] for start in starts])
    core = lax.axis_index("core")
    pad = jnp.zeros((quarter, HD), BF)
    queries = [jnp.concatenate([q * BF(1.0 / math.sqrt(HD)), pad], axis=1) for q, _, _ in halves]
    mine_out_ref[...] = jnp.where(core == 0, queries[0], queries[1])
    other_ref[...] = jnp.where(core == 0, queries[1], queries[0])
    for which in range(2):
        kv = jnp.concatenate(halves[which][1:], axis=1)
        for chip in range(ckv_ref.shape[0] // 2):
            ckv_ref[2 * chip + which] = kv


def chip_kernel(mine_ref, other_ref, out_ref):
    count = mine_ref.shape[0]
    out_ref[:count, :] = mine_ref[...]
    out_ref[count:, :] = other_ref[...]


def coarse_kernel(kv_ref, *refs):
    blocks, out_ref = refs[:-1], refs[-1]
    count = out_ref.shape[1]
    halves = []
    for number, block in enumerate(blocks):
        away = 4 if number > 6 else (number + 1) // 2 if number % 2 else -(number // 2)
        if number > 6:
            halves.append((away, number - 7, block, 0))
        else:
            halves += [(away, 0, block, 0), (away, 1, block, count)]
    group = 4
    rows = group * count
    lane = iota((rows, 128), 1)
    low = lane < HD
    part, slot = lane >> 3, lane & 7
    ones = jnp.ones((kv_ref.shape[0], 128), BF)
    z, core = lax.axis_index("zh") * 4 + lax.axis_index("zl"), lax.axis_index("core")
    for start in range(0, len(halves), group):
        here = halves[start : start + group]
        q2 = jnp.concatenate([block[at : at + count, :128] for _, _, block, at in here], axis=0)
        q3 = jnp.concatenate([block[at : at + count, 128:] for _, _, block, at in here], axis=0)
        zero = jnp.zeros_like(q2)
        parts = ((jnp.where(low, q2, zero), 0, 128), (jnp.where(low, zero, q2), 0, 256), (q3, 128, 256))
        stats = jnp.zeros((rows, 128), F32)
        accs = []
        for head, (query, key_at, value_at) in enumerate(parts):
            score = dot_t(query, kv_ref[:, key_at : key_at + 128])
            top = jnp.max(score, axis=1, keepdims=True)
            values = jnp.concatenate([kv_ref[:, value_at : value_at + 128], ones], axis=1)
            both = dot(jnp.exp(score - top).astype(BF), values)
            accs.append(both[:, :128])
            stats = jnp.where((slot == head) & (part < 3), top, stats)
            stats = jnp.where((slot == head) & (part >= 3), both[:, 128:], stats)
        high = stats.astype(BF).astype(F32)
        middle = (stats - high).astype(BF).astype(F32)
        last = stats - high - middle
        stats = jnp.where((part == 0) | (part == 3), high, jnp.where((part == 1) | (part == 4), middle, last))
        left = jnp.where(low, accs[1], accs[2]).astype(BF)
        right = jnp.where(low, stats, accs[0]).astype(BF)
        for k, (away, other, _, _) in enumerate(here):
            to = (z + away + 8) % 8
            at = ((to % 4) * 2 + to // 4) * 2 + (core + other) % 2
            out_ref[at, :, :128] = left[k * count : (k + 1) * count]
            out_ref[at, :, 128:] = right[k * count : (k + 1) * count]


def finish_kernel(states_ref, coarse_ref, mid_ref, w_cout_ref, w_up_ref, out_ref):
    sources, count, _ = states_ref.shape
    row, column = iota((128, 256), 0), iota((128, 256), 1)
    head = jnp.where(column < HD, 1, jnp.where(column < 2 * HD, 2, 0))
    part, slot = row >> 3, row & 7
    stats = states_ref[:, :, 128:].reshape(sources * count, 128)
    tops = dot(stats, one_hot((slot == head) & (part < 3))).reshape(sources, count, 256)
    totals = dot(stats, one_hot((slot == head) & (part >= 3) & (part < 5))).reshape(sources, count, 256)
    cattn = []
    for core in range(2):
        mine = range(core, sources, 2)
        best = functools.reduce(jnp.maximum, [tops[source] for source in mine])
        factors = [jnp.exp(tops[source] - best) for source in mine]
        total = sum(totals[source] * factor for source, factor in zip(mine, factors))
        acc = sum(states_ref[source].astype(F32) * factor for source, factor in zip(mine, factors))
        value = (acc / total).astype(BF)
        cattn += [value[:, 3 * HD :], value[:, : 2 * HD]]
    attended = dot(jnp.concatenate(cattn, axis=1), w_cout_ref[...])
    coarse_mid = (coarse_ref[...].astype(F32) + attended).astype(BF)
    upper = dot(coarse_mid, w_up_ref[...])
    upper = jnp.concatenate([upper[:, part * D : (part + 1) * D] for part in range(4)], axis=0)
    fine = (mid_ref[...].astype(F32) + upper).astype(BF)
    out_ref[...] = dot(one_hot(natural_of(iota((N, N), 1)) == iota((N, N), 0)), fine).astype(BF)


def call(kernel, outs, scratch=(), smem=0, micros=0):
    vmem = pl.BlockSpec(memory_space=pltpu.VMEM)
    cost = pl.CostEstimate(flops=micros * 10**9, transcendentals=0, bytes_accessed=micros << 21) if micros else None

    def run(*args):
        return pl.pallas_call(
            kernel,
            out_shape=[jax.ShapeDtypeStruct(shape, BF if kind is None else kind) for shape, kind in outs],
            in_specs=[pl.BlockSpec(memory_space=pltpu.SMEM)] * smem + [vmem] * (len(args) - smem),
            out_specs=[vmem] * len(outs),
            scratch_shapes=list(scratch),
            cost_estimate=cost,
            compiler_params=pltpu.CompilerParams(vmem_limit_bytes=40 * 1024 * 1024),
        )(*args)

    return run


def permuted(value, target):
    pairs = []
    for at in itertools.product(*(range(size) for size in SIZES)):
        to = target(*at)
        if to is not None:
            pairs.append((int(np.ravel_multi_index(at, SIZES)), int(np.ravel_multi_index(to, SIZES))))
    return lax.ppermute(value, AXES, pairs)


def partner(index, far):
    other = index ^ 1 if not far else (index + 1 if index % 2 else index - 1)
    return other if 0 <= other < 16 else None


def row_partner(far):
    def target(zl, y, zh, x, core):
        to = partner(zl * 4 + y, far)
        return None if to is None else (to // 4, to % 4, zh, x, core)

    return target


def col_partner(far):
    def target(zl, y, zh, x, core):
        to = partner(zh * 8 + x * 2 + core, far)
        return None if to is None else (zl, y, to // 8, to // 2 % 4, to % 2)

    return target


def along_z(step):
    def target(zl, y, zh, x, core):
        z = (zh * 4 + zl + step) % 8
        return (z % 4, y, z // 4, x, core)

    return target


def other_core(zl, y, zh, x, core):
    return (zl, y, zh, x, 1 - core)


def per_device(tokens, stale_kv, timestep, w_time, w_qkv, w_out, w_merge, w_cqkv, w_cout, w_up):
    width, coarse_width = w_cout.shape
    count = N // 4
    band = ((3, SIDE, 2 * D), None)
    row_near, row_far = call(rows_kernel, [band, band], micros=4)(stale_kv)
    row_near = permuted(row_near, row_partner(False))
    row_far = permuted(row_far, row_partner(True))
    query, kv, fresh_kv, gate, mine = call(
        project_kernel,
        [((N, D), None), ((N, 2 * D), None), ((N, 2 * D), None), ((8, D), F32), ((N, D), None)],
        smem=1,
        micros=8,
    )(timestep, tokens.reshape(N, D), w_time, w_qkv)
    col_near, col_far = call(columns_kernel, [((EDGE, 2 * D), None)] * 2, micros=2)(stale_kv, row_near, row_far)
    col_near = permuted(col_near, col_partner(False))
    col_far = permuted(col_far, col_partner(True))
    mid, coarse, cq, other, ckv = call(
        fine_kernel,
        [((N, D), None), ((count, coarse_width), None), ((count, 256), None), ((count, 256), None), ((32, count, width), None)],
        scratch=[pltpu.VMEM((N, 2 * D), BF)],
        micros=3,
    )(query, kv, gate, mine, row_near, row_far, col_near, col_far, w_out, w_merge, w_cqkv)
    ckv = lax.all_to_all(ckv, ("y", "x", "core"), 0, 0)
    other = permuted(other, other_core)
    (block,) = call(chip_kernel, [((2 * count, 256), None)])(cq, other)
    up = down = block
    blocks = [block]
    for _ in range(3):
        up, down = permuted(up, along_z(-1)), permuted(down, along_z(1))
        blocks += [up, down]
    blocks += [permuted(up[:count], along_z(-1)), permuted(down[count:], along_z(1))]
    (states,) = call(coarse_kernel, [((16, count, 256), None)], micros=9)(ckv.reshape(32 * count, width), *blocks)
    states = lax.all_to_all(states, ("zl", "zh", "core"), 0, 0)
    (fine_out,) = call(finish_kernel, [((N, D), None)], micros=2)(states, coarse, mid, w_cout, w_up)
    return (fine_out.reshape(SIDE, SIDE, D), fresh_kv.reshape(SIDE, SIDE, 2 * D))


def solution(mesh):
    fine = Mesh(mesh.devices.reshape(SIZES), AXES)
    tiled = P(("zl", "y"), ("zh", "x", "core"), None)
    return jax.shard_map(
        per_device,
        mesh=fine,
        in_specs=(tiled, tiled) + (P(),) * 8,
        out_specs=(tiled, tiled),
        check_vma=False,
    )
```

```python
import functools
import itertools
import math

import jax
import jax.numpy as jnp
import numpy as np
from jax import lax
from jax.experimental import pallas as pl
from jax.experimental.pallas import tpu as pltpu
from jax.sharding import Mesh
from jax.sharding import PartitionSpec as P

HD = 64
SIDE = 16
N = SIDE * SIDE
D = 256
BAND = 3 * SIDE
EDGE = 80
BF = jnp.bfloat16
F32 = jnp.float32
AXES = ("zl", "y", "zh", "x", "core")
SIZES = (4, 4, 2, 4, 2)


def dot(a, b):
    return lax.dot_general(a, b, (((1,), (0,)), ((), ())), preferred_element_type=F32)


def dot_t(a, b):
    return lax.dot_general(a, b, (((1,), (1,)), ((), ())), preferred_element_type=F32)


def one_hot(condition):
    return condition.astype(F32).astype(BF)


def iota(shape, dim):
    return lax.broadcasted_iota(jnp.int32, shape, dim)


def tile_row():
    return lax.axis_index("zl") * 4 + lax.axis_index("y")


def tile_col():
    return lax.axis_index("zh") * 8 + lax.axis_index("x") * 2 + lax.axis_index("core")


def third(n):
    return (n * 171) >> 9


def layer_norm(values):
    values = values.astype(F32)
    mean = jnp.mean(values, axis=-1, keepdims=True)
    centred = values - mean
    var = jnp.mean(centred * centred, axis=-1, keepdims=True)
    return centred * lax.rsqrt(var + 1e-06)


def natural_of(m):
    a, b, r, c = m >> 7, (m >> 6) & 1, (m >> 3) & 7, m & 7
    return (2 * r + a) * SIDE + 2 * c + b


def rows_kernel(stale_ref, near_ref, far_ref):
    odd = tile_row() % 2
    near_ref[...] = stale_ref[pl.ds((1 - odd) * 13, 3)]
    far_ref[...] = stale_ref[pl.ds(odd * 13, 3)]


def columns_kernel(stale_ref, row_near_ref, row_far_ref, near_ref, far_ref):
    odd = tile_col() % 2
    stale = stale_ref[...].reshape(N, 2 * D)
    row_near = row_near_ref[...].reshape(BAND, 2 * D)
    row_far = row_far_ref[...].reshape(BAND, 2 * D)
    for out, first in ((near_ref, (1 - odd) * 13), (far_ref, odd * 13)):
        take, source = iota((BAND, N), 0), iota((BAND, N), 1)
        i = third(take)
        out[:BAND, :] = dot(one_hot(source == i * SIDE + first + take - 3 * i), stale).astype(BF)
        take, source = iota((SIDE, BAND), 0), iota((SIDE, BAND), 1)
        i = third(take)
        corner = one_hot((source == i * SIDE + first + take - 3 * i) & (take < 9))
        out[BAND : BAND + SIDE, :] = dot(corner, row_near).astype(BF)
        out[BAND + SIDE :, :] = dot(corner, row_far).astype(BF)


def project_kernel(time_ref, tokens_ref, w_time_ref, w_qkv_ref, q_ref, kv_ref, kv_out_ref, gate_ref, mine_ref):
    half = D // 2
    index = iota((8, half), 1).astype(F32)
    angle = time_ref[0].astype(F32) * jnp.exp(-math.log(10000.0) * index * 2.0 / D)
    emb = jnp.concatenate([jnp.cos(angle), jnp.sin(angle)], axis=1)
    act = (emb / (1.0 + jnp.exp(-emb))).astype(BF)
    mod = dot(act, w_time_ref[...])
    gate_ref[...] = mod[:, 2 * D :]
    regroup = one_hot(natural_of(iota((N, N), 0)) == iota((N, N), 1))
    tokens = tokens_ref[...]
    mine_ref[...] = dot(regroup, tokens).astype(BF)
    normed = (layer_norm(tokens) * (1.0 + mod[0:1, D : 2 * D]) + mod[0:1, :D]).astype(BF)
    kv = dot(normed, w_qkv_ref[:, D:]).astype(BF)
    kv_ref[...] = kv
    kv_out_ref[...] = kv
    q_ref[...] = dot(dot(regroup, normed).astype(BF), w_qkv_ref[:, :D]).astype(BF)


def fine_kernel(q_ref, kv_ref, gate_ref, mine_ref, row_near_ref, row_far_ref, col_near_ref, col_far_ref,
                w_out_ref, w_merge_ref, w_cqkv_ref,
                mid_ref, coarse_ref, mine_out_ref, other_ref, ckv_ref, halo):
    halo[:BAND, :] = row_near_ref[...].reshape(BAND, 2 * D)
    halo[BAND : 2 * BAND, :] = row_far_ref[...].reshape(BAND, 2 * D)
    halo[2 * BAND : 2 * BAND + EDGE, :] = col_near_ref[...]
    halo[2 * BAND + EDGE :, :] = col_far_ref[...]

    row, col = tile_row(), tile_col()
    row_odd, col_odd = row % 2, col % 2

    def after(odd):
        return (1 - odd) * SIDE - 3 * odd

    near_i, far_i = after(row_odd), after(1 - row_odd)
    near_j, far_j = after(col_odd), after(1 - col_odd)
    k = iota((1, N), 1)
    own_i, own_j = k >> 4, k & 15
    edge = jnp.where(k >= 2 * BAND + EDGE, k - 2 * BAND - EDGE, k - 2 * BAND)
    edge = jnp.maximum(edge, 0)
    cut = jnp.where(edge < BAND, edge, (edge - BAND) & 15)
    step = third(cut)
    side_i = jnp.where(edge < BAND, step, jnp.where(edge < BAND + SIDE, near_i, far_i) + step)
    side_j = jnp.where(k >= 2 * BAND + EDGE, far_j, near_j) + cut - 3 * step
    side_i = jnp.where((edge >= BAND) & (cut >= 9), -1000, side_i)
    band = jnp.where(k >= BAND, k - BAND, k)
    band_i = jnp.where(k >= BAND, far_i, near_i) + (band >> 4)
    halo_i = jnp.where(k < 2 * BAND, band_i, side_i)
    halo_j = jnp.where(k < 2 * BAND, band & 15, side_j)
    ki = jnp.concatenate([own_i, halo_i], axis=1)
    kj = jnp.concatenate([own_j, halo_j], axis=1)
    at_i, at_j = ki + row * SIDE, kj + col * SIDE
    in_image = (at_i >= 0) & (at_i < 16 * SIDE) & (at_j >= 0) & (at_j < 16 * SIDE)
    ki = jnp.where(in_image, ki, -1000)
    natural = natural_of(iota((N, 1), 0))
    near = (jnp.abs((natural >> 4) - ki) <= 3) & (jnp.abs((natural & 15) - kj) <= 3)

    lane = iota((N, 128), 1)
    attn = []
    for pair in range(D // 128):
        cols = slice(pair * 128, pair * 128 + 128)
        vcols = slice(D + pair * 128, D + pair * 128 + 128)
        q2 = q_ref[:, cols]
        halves = []
        for which in range(2):
            q1 = jnp.where((lane < HD) if which == 0 else (lane >= HD), q2, jnp.zeros_like(q2))
            score = jnp.concatenate([dot_t(q1, kv_ref[:, cols]), dot_t(q1, halo[:, cols])], axis=1)
            score = jnp.where(near, score * (1.0 / math.sqrt(HD)), -1e30)
            expo = jnp.exp(score - jnp.max(score, axis=1, keepdims=True))
            total = jnp.sum(expo, axis=1, keepdims=True)
            weights = expo.astype(BF)
            acc = dot(weights[:, :N], kv_ref[:, vcols]) + dot(weights[:, N:], halo[:, vcols])
            halves.append(acc / total)
        attn.append(jnp.where(lane < HD, halves[0], halves[1]).astype(BF))
    attn = jnp.concatenate(attn, axis=1)
    mid = (mine_ref[...].astype(F32) + gate_ref[0:1, :] * dot(attn, w_out_ref[...])).astype(BF)
    mid_ref[...] = mid
    quarter = N // 4
    coarse = sum(
        dot(mid[part * quarter : (part + 1) * quarter, :], w_merge_ref[part * D : (part + 1) * D, :])
        for part in range(4)
    ).astype(BF)
    coarse_ref[...] = coarse
    cqkv = dot(layer_norm(coarse).astype(BF), w_cqkv_ref[...]).astype(BF)
    width = w_cqkv_ref.shape[1] // 3
    half = width // 2
    halves = []
    for which in range(2):
        starts = [part * width + which * half for part in range(3)]
        halves.append([cqkv[:, start : start + half] for start in starts])
    core = lax.axis_index("core")
    pad = jnp.zeros((quarter, HD), BF)
    queries = [jnp.concatenate([q * BF(1.0 / math.sqrt(HD)), pad], axis=1) for q, _, _ in halves]
    mine_out_ref[...] = jnp.where(core == 0, queries[0], queries[1])
    other_ref[...] = jnp.where(core == 0, queries[1], queries[0])
    for which in range(2):
        kv = jnp.concatenate(halves[which][1:], axis=1)
        for chip in range(ckv_ref.shape[0] // 2):
            ckv_ref[2 * chip + which] = kv


def chip_kernel(mine_ref, other_ref, out_ref):
    count = mine_ref.shape[0]
    out_ref[:count, :] = mine_ref[...]
    out_ref[count:, :] = other_ref[...]


def coarse_kernel(kv_ref, queries_ref, *rest):
    out_ref = rest[-1]
    queries = queries_ref[...]
    rows = queries.shape[0]
    lane = iota((rows, 128), 1)
    low = lane < HD
    part, slot = lane >> 3, lane & 7
    ones = jnp.ones((kv_ref.shape[0], 128), BF)
    q2, q3 = queries[:, :128], queries[:, 128:]
    zero = jnp.zeros_like(q2)
    parts = ((jnp.where(low, q2, zero), 0, 128), (jnp.where(low, zero, q2), 0, 256), (q3, 128, 256))
    stats = jnp.zeros((rows, 128), F32)
    accs = []
    for head, (query, key_at, value_at) in enumerate(parts):
        score = dot_t(query, kv_ref[:, key_at : key_at + 128])
        top = jnp.max(score, axis=1, keepdims=True)
        values = jnp.concatenate([kv_ref[:, value_at : value_at + 128], ones], axis=1)
        both = dot(jnp.exp(score - top).astype(BF), values)
        accs.append(both[:, :128])
        stats = jnp.where((slot == head) & (part < 3), top, stats)
        stats = jnp.where((slot == head) & (part >= 3), both[:, 128:], stats)
    out_ref[:, :128] = jnp.where(low, accs[1], accs[2]).astype(BF)
    out_ref[:, 128:] = jnp.where(low, split(stats, part), accs[0]).astype(BF)


def split(stats, part):
    high = stats.astype(BF).astype(F32)
    middle = (stats - high).astype(BF).astype(F32)
    last = stats - high - middle
    return jnp.where((part == 0) | (part == 3), high, jnp.where((part == 1) | (part == 4), middle, last))


def merged(states):
    row, column = iota((128, 256), 0), iota((128, 256), 1)
    head = jnp.where(column < HD, 1, jnp.where(column < 2 * HD, 2, 0))
    part, slot = row >> 3, row & 7
    pick_top = one_hot((slot == head) & (part < 3))
    pick_total = one_hot((slot == head) & (part >= 3) & (part < 5))
    tops = [dot(state[:, 128:], pick_top) for state in states]
    best = functools.reduce(jnp.maximum, tops)
    factors = [jnp.exp(top - best) for top in tops]
    total = sum(dot(state[:, 128:], pick_total) * factor for state, factor in zip(states, factors))
    acc = sum(state.astype(F32) * factor for state, factor in zip(states, factors))
    return best, total, acc


def pair_kernel(*refs):
    states, out_ref = refs[:-1], refs[-1]
    count = out_ref.shape[0]
    best, total, acc = merged([state[count:, :] for state in states])
    lane = iota((count, 128), 1)
    part, slot = lane >> 3, lane & 7
    stats = jnp.zeros((count, 128), F32)
    for head, column in enumerate((128, 0, HD)):
        stats = jnp.where((slot == head) & (part < 3), best[:, column : column + 1], stats)
        stats = jnp.where((slot == head) & (part >= 3), total[:, column : column + 1], stats)
    out_ref[:, :128] = acc[:, :128].astype(BF)
    out_ref[:, 128:] = jnp.where(lane < HD, split(stats, part), acc[:, 128:]).astype(BF)


def merge_kernel(*refs):
    states, far_ref, mine_ref, other_ref = refs[:-3], refs[-3], refs[-2], refs[-1]
    count = far_ref.shape[0]
    best, total, acc = merged([state[:count, :] for state in states] + [far_ref[...]])
    cattn = (acc / total).astype(BF)
    cattn = jnp.concatenate([cattn[:, 3 * HD :], cattn[:, : 2 * HD]], axis=1)
    mine_ref[...] = cattn[: count // 2]
    other_ref[...] = cattn[count // 2 :]


def finish_kernel(mine_ref, other_ref, coarse_ref, mid_ref, w_cout_ref, w_up_ref, out_ref):
    half = mine_ref.shape[1]
    core = lax.axis_index("core")
    attended = dot(mine_ref[...], w_cout_ref[pl.ds(pl.multiple_of(core * half, half), half), :])
    attended += dot(other_ref[...], w_cout_ref[pl.ds(pl.multiple_of((1 - core) * half, half), half), :])
    coarse_mid = (coarse_ref[...].astype(F32) + attended).astype(BF)
    upper = dot(coarse_mid, w_up_ref[...])
    upper = jnp.concatenate([upper[:, part * D : (part + 1) * D] for part in range(4)], axis=0)
    fine = (mid_ref[...].astype(F32) + upper).astype(BF)
    out_ref[...] = dot(one_hot(natural_of(iota((N, N), 1)) == iota((N, N), 0)), fine).astype(BF)


def call(kernel, outs, scratch=(), smem=0, micros=0, short=False):
    vmem = pl.BlockSpec(memory_space=pltpu.VMEM)
    cost = pl.CostEstimate(flops=micros * 10**9, transcendentals=0, bytes_accessed=micros << 21) if micros else None
    if short:
        cost = pl.CostEstimate(flops=1000, transcendentals=0, bytes_accessed=1000)

    def run(*args):
        return pl.pallas_call(
            kernel,
            out_shape=[jax.ShapeDtypeStruct(shape, BF if kind is None else kind) for shape, kind in outs],
            in_specs=[pl.BlockSpec(memory_space=pltpu.SMEM)] * smem + [vmem] * (len(args) - smem),
            out_specs=[vmem] * len(outs),
            scratch_shapes=list(scratch),
            cost_estimate=cost,
            compiler_params=pltpu.CompilerParams(vmem_limit_bytes=40 * 1024 * 1024),
        )(*args)

    return run


def permuted(value, target):
    pairs = []
    for at in itertools.product(*(range(size) for size in SIZES)):
        to = target(*at)
        if to is not None:
            pairs.append((int(np.ravel_multi_index(at, SIZES)), int(np.ravel_multi_index(to, SIZES))))
    return lax.ppermute(value, AXES, pairs)


def partner(index, far):
    other = index ^ 1 if not far else (index + 1 if index % 2 else index - 1)
    return other if 0 <= other < 16 else None


def row_partner(far):
    def target(zl, y, zh, x, core):
        to = partner(zl * 4 + y, far)
        return None if to is None else (to // 4, to % 4, zh, x, core)

    return target


def col_partner(far):
    def target(zl, y, zh, x, core):
        to = partner(zh * 8 + x * 2 + core, far)
        return None if to is None else (zl, y, to // 8, to // 2 % 4, to % 2)

    return target


def along_z(step):
    def target(zl, y, zh, x, core):
        z = (zh * 4 + zl) ^ step
        return (z % 4, y, z // 4, x, core)

    return target


def other_core(zl, y, zh, x, core):
    return (zl, y, zh, x, 1 - core)


def per_device(tokens, stale_kv, timestep, w_time, w_qkv, w_out, w_merge, w_cqkv, w_cout, w_up):
    width, coarse_width = w_cout.shape
    count = N // 4
    band = ((3, SIDE, 2 * D), None)
    row_near, row_far = call(rows_kernel, [band, band], micros=4)(stale_kv)
    row_near = permuted(row_near, row_partner(False))
    row_far = permuted(row_far, row_partner(True))
    query, kv, fresh_kv, gate, mine = call(
        project_kernel,
        [((N, D), None), ((N, 2 * D), None), ((N, 2 * D), None), ((8, D), F32), ((N, D), None)],
        smem=1,
        micros=8,
    )(timestep, tokens.reshape(N, D), w_time, w_qkv)
    col_near, col_far = call(columns_kernel, [((EDGE, 2 * D), None)] * 2, micros=2)(stale_kv, row_near, row_far)
    col_near = permuted(col_near, col_partner(False))
    col_far = permuted(col_far, col_partner(True))
    mid, coarse, cq, other, ckv = call(
        fine_kernel,
        [((N, D), None), ((count, coarse_width), None), ((count, 256), None), ((count, 256), None), ((32, count, width), None)],
        scratch=[pltpu.VMEM((N, 2 * D), BF)],
        micros=3,
    )(query, kv, gate, mine, row_near, row_far, col_near, col_far, w_out, w_merge, w_cqkv)
    ckv = lax.all_to_all(ckv, ("y", "x", "core"), 0, 0)
    other = permuted(other, other_core)
    (block,) = call(chip_kernel, [((2 * count, 256), None)])(cq, other)
    block = jnp.concatenate([block, permuted(block, along_z(1))], axis=0)
    blocks = {step: permuted(block, along_z(step)) for step in (4, 2, 6)}
    keys_values = ckv.reshape(32 * count, width)
    states = []
    for step in (4, 2, 6, 0):
        early = states[: max(0, len(states) - 1)] if step == 0 else []
        (state,) = call(coarse_kernel, [((4 * count, 256), None)], short=True)(keys_values, blocks.get(step, block), *early)
        states.append(permuted(state, along_z(step)) if step else state)
    (far,) = call(pair_kernel, [((2 * count, 256), None)])(*states)
    far = permuted(far, along_z(1))
    attn, other = call(merge_kernel, [((count, width // 2), None)] * 2)(*states, far)
    other = permuted(other, other_core)
    (fine_out,) = call(finish_kernel, [((N, D), None)], micros=2)(attn, other, coarse, mid, w_cout, w_up)
    return (fine_out.reshape(SIDE, SIDE, D), fresh_kv.reshape(SIDE, SIDE, 2 * D))


def solution(mesh):
    fine = Mesh(mesh.devices.reshape(SIZES), AXES)
    tiled = P(("zl", "y"), ("zh", "x", "core"), None)
    return jax.shard_map(
        per_device,
        mesh=fine,
        in_specs=(tiled, tiled) + (P(),) * 8,
        out_specs=(tiled, tiled),
        check_vma=False,
    )
```

```python
import functools
import itertools
import math

import jax
import jax.numpy as jnp
import numpy as np
from jax import lax
from jax.experimental import pallas as pl
from jax.experimental.pallas import tpu as pltpu
from jax.sharding import Mesh
from jax.sharding import PartitionSpec as P

HD = 64
SIDE = 16
N = SIDE * SIDE
D = 256
BAND = 3 * SIDE
EDGE = 80
BF = jnp.bfloat16
F32 = jnp.float32
AXES = ("zl", "y", "zh", "x", "core")
SIZES = (4, 4, 2, 4, 2)


def dot(a, b):
    return lax.dot_general(a, b, (((1,), (0,)), ((), ())), preferred_element_type=F32)


def dot_t(a, b):
    return lax.dot_general(a, b, (((1,), (1,)), ((), ())), preferred_element_type=F32)


def one_hot(condition):
    return condition.astype(F32).astype(BF)


def iota(shape, dim):
    return lax.broadcasted_iota(jnp.int32, shape, dim)


def tile_row():
    return lax.axis_index("zl") * 4 + lax.axis_index("y")


def tile_col():
    return lax.axis_index("zh") * 8 + lax.axis_index("x") * 2 + lax.axis_index("core")


def third(n):
    return (n * 171) >> 9


def layer_norm(values):
    values = values.astype(F32)
    mean = jnp.mean(values, axis=-1, keepdims=True)
    centred = values - mean
    var = jnp.mean(centred * centred, axis=-1, keepdims=True)
    return centred * lax.rsqrt(var + 1e-06)


def natural_of(m):
    a, b, r, c = m >> 7, (m >> 6) & 1, (m >> 3) & 7, m & 7
    return (2 * r + a) * SIDE + 2 * c + b


def rows_kernel(stale_ref, near_ref, far_ref):
    odd = tile_row() % 2
    near_ref[...] = stale_ref[pl.ds((1 - odd) * 13, 3)]
    far_ref[...] = stale_ref[pl.ds(odd * 13, 3)]


def columns_kernel(stale_ref, row_near_ref, row_far_ref, near_ref, far_ref):
    odd = tile_col() % 2
    stale = stale_ref[...].reshape(N, 2 * D)
    row_near = row_near_ref[...].reshape(BAND, 2 * D)
    row_far = row_far_ref[...].reshape(BAND, 2 * D)
    for out, first in ((near_ref, (1 - odd) * 13), (far_ref, odd * 13)):
        take, source = iota((BAND, N), 0), iota((BAND, N), 1)
        i = third(take)
        out[:BAND, :] = dot(one_hot(source == i * SIDE + first + take - 3 * i), stale).astype(BF)
        take, source = iota((SIDE, BAND), 0), iota((SIDE, BAND), 1)
        i = third(take)
        corner = one_hot((source == i * SIDE + first + take - 3 * i) & (take < 9))
        out[BAND : BAND + SIDE, :] = dot(corner, row_near).astype(BF)
        out[BAND + SIDE :, :] = dot(corner, row_far).astype(BF)


def project_kernel(time_ref, tokens_ref, w_time_ref, w_qkv_ref, q_ref, kv_ref, kv_out_ref, gate_ref, mine_ref):
    half = D // 2
    index = iota((8, half), 1).astype(F32)
    angle = time_ref[0].astype(F32) * jnp.exp(-math.log(10000.0) * index * 2.0 / D)
    emb = jnp.concatenate([jnp.cos(angle), jnp.sin(angle)], axis=1)
    act = (emb / (1.0 + jnp.exp(-emb))).astype(BF)
    mod = dot(act, w_time_ref[...])
    gate_ref[...] = mod[:, 2 * D :]
    regroup = one_hot(natural_of(iota((N, N), 0)) == iota((N, N), 1))
    tokens = tokens_ref[...]
    mine_ref[...] = dot(regroup, tokens).astype(BF)
    normed = (layer_norm(tokens) * (1.0 + mod[0:1, D : 2 * D]) + mod[0:1, :D]).astype(BF)
    kv = dot(normed, w_qkv_ref[:, D:]).astype(BF)
    kv_ref[...] = kv
    kv_out_ref[...] = kv
    q_ref[...] = dot(dot(regroup, normed).astype(BF), w_qkv_ref[:, :D]).astype(BF)


def fine_kernel(q_ref, kv_ref, gate_ref, mine_ref, row_near_ref, row_far_ref, col_near_ref, col_far_ref,
                w_out_ref, w_merge_ref, w_cqkv_ref,
                mid_ref, coarse_ref, mine_out_ref, other_ref, ckv_ref, halo):
    halo[:BAND, :] = row_near_ref[...].reshape(BAND, 2 * D)
    halo[BAND : 2 * BAND, :] = row_far_ref[...].reshape(BAND, 2 * D)
    halo[2 * BAND : 2 * BAND + EDGE, :] = col_near_ref[...]
    halo[2 * BAND + EDGE :, :] = col_far_ref[...]

    row, col = tile_row(), tile_col()
    row_odd, col_odd = row % 2, col % 2

    def after(odd):
        return (1 - odd) * SIDE - 3 * odd

    near_i, far_i = after(row_odd), after(1 - row_odd)
    near_j, far_j = after(col_odd), after(1 - col_odd)
    k = iota((1, N), 1)
    own_i, own_j = k >> 4, k & 15
    edge = jnp.where(k >= 2 * BAND + EDGE, k - 2 * BAND - EDGE, k - 2 * BAND)
    edge = jnp.maximum(edge, 0)
    cut = jnp.where(edge < BAND, edge, (edge - BAND) & 15)
    step = third(cut)
    side_i = jnp.where(edge < BAND, step, jnp.where(edge < BAND + SIDE, near_i, far_i) + step)
    side_j = jnp.where(k >= 2 * BAND + EDGE, far_j, near_j) + cut - 3 * step
    side_i = jnp.where((edge >= BAND) & (cut >= 9), -1000, side_i)
    band = jnp.where(k >= BAND, k - BAND, k)
    band_i = jnp.where(k >= BAND, far_i, near_i) + (band >> 4)
    halo_i = jnp.where(k < 2 * BAND, band_i, side_i)
    halo_j = jnp.where(k < 2 * BAND, band & 15, side_j)
    ki = jnp.concatenate([own_i, halo_i], axis=1)
    kj = jnp.concatenate([own_j, halo_j], axis=1)
    at_i, at_j = ki + row * SIDE, kj + col * SIDE
    in_image = (at_i >= 0) & (at_i < 16 * SIDE) & (at_j >= 0) & (at_j < 16 * SIDE)
    ki = jnp.where(in_image, ki, -1000)
    natural = natural_of(iota((N, 1), 0))
    near = (jnp.abs((natural >> 4) - ki) <= 3) & (jnp.abs((natural & 15) - kj) <= 3)

    lane = iota((N, 128), 1)
    attn = []
    for pair in range(D // 128):
        cols = slice(pair * 128, pair * 128 + 128)
        vcols = slice(D + pair * 128, D + pair * 128 + 128)
        q2 = q_ref[:, cols]
        halves = []
        for which in range(2):
            q1 = jnp.where((lane < HD) if which == 0 else (lane >= HD), q2, jnp.zeros_like(q2))
            score = jnp.concatenate([dot_t(q1, kv_ref[:, cols]), dot_t(q1, halo[:, cols])], axis=1)
            score = jnp.where(near, score * (1.0 / math.sqrt(HD)), -1e30)
            expo = jnp.exp(score - jnp.max(score, axis=1, keepdims=True))
            total = jnp.sum(expo, axis=1, keepdims=True)
            weights = expo.astype(BF)
            acc = dot(weights[:, :N], kv_ref[:, vcols]) + dot(weights[:, N:], halo[:, vcols])
            halves.append(acc / total)
        attn.append(jnp.where(lane < HD, halves[0], halves[1]).astype(BF))
    attn = jnp.concatenate(attn, axis=1)
    mid = (mine_ref[...].astype(F32) + gate_ref[0:1, :] * dot(attn, w_out_ref[...])).astype(BF)
    mid_ref[...] = mid
    quarter = N // 4
    coarse = sum(
        dot(mid[part * quarter : (part + 1) * quarter, :], w_merge_ref[part * D : (part + 1) * D, :])
        for part in range(4)
    ).astype(BF)
    coarse_ref[...] = coarse
    cqkv = dot(layer_norm(coarse).astype(BF), w_cqkv_ref[...]).astype(BF)
    width = w_cqkv_ref.shape[1] // 3
    half = width // 2
    halves = []
    for which in range(2):
        starts = [part * width + which * half for part in range(3)]
        halves.append([cqkv[:, start : start + half] for start in starts])
    core = lax.axis_index("core")
    pad = jnp.zeros((quarter, HD), BF)
    queries = [jnp.concatenate([q * BF(1.0 / math.sqrt(HD)), pad], axis=1) for q, _, _ in halves]
    mine_out_ref[...] = jnp.where(core == 0, queries[0], queries[1])
    other_ref[...] = jnp.where(core == 0, queries[1], queries[0])
    for which in range(2):
        ckv_ref[which] = jnp.concatenate(halves[which][1:], axis=1)
    for block in range(2, ckv_ref.shape[0]):
        ckv_ref[block] = ckv_ref[block % 2]


def chip_kernel(mine_ref, other_ref, out_ref):
    count = mine_ref.shape[0]
    out_ref[:count, :] = mine_ref[...]
    out_ref[count:, :] = other_ref[...]


def coarse_kernel(kv_ref, queries_ref, *rest):
    out_ref = rest[-1]
    queries = queries_ref[...]
    rows = queries.shape[0]
    lane = iota((rows, 128), 1)
    low = lane < HD
    part, slot = lane >> 3, lane & 7
    ones = jnp.ones((kv_ref.shape[0], 128), BF)
    q2, q3 = queries[:, :128], queries[:, 128:]
    zero = jnp.zeros_like(q2)
    parts = ((jnp.where(low, q2, zero), 0, 128), (jnp.where(low, zero, q2), 0, 256), (q3, 128, 256))
    stats = jnp.zeros((rows, 128), F32)
    accs = []
    for head, (query, key_at, value_at) in enumerate(parts):
        score = dot_t(query, kv_ref[:, key_at : key_at + 128])
        top = jnp.max(score, axis=1, keepdims=True)
        values = jnp.concatenate([kv_ref[:, value_at : value_at + 128], ones], axis=1)
        both = dot(jnp.exp(score - top).astype(BF), values)
        accs.append(both[:, :128])
        stats = jnp.where((slot == head) & (part < 3), top, stats)
        stats = jnp.where((slot == head) & (part >= 3), both[:, 128:], stats)
    out_ref[:, :128] = jnp.where(low, accs[1], accs[2]).astype(BF)
    out_ref[:, 128:] = jnp.where(low, split(stats, part), accs[0]).astype(BF)


def split(stats, part):
    high = stats.astype(BF).astype(F32)
    middle = (stats - high).astype(BF).astype(F32)
    last = stats - high - middle
    return jnp.where((part == 0) | (part == 3), high, jnp.where((part == 1) | (part == 4), middle, last))


def merged(states):
    row, column = iota((128, 256), 0), iota((128, 256), 1)
    head = jnp.where(column < HD, 1, jnp.where(column < 2 * HD, 2, 0))
    part, slot = row >> 3, row & 7
    pick_top = one_hot((slot == head) & (part < 3))
    pick_total = one_hot((slot == head) & (part >= 3) & (part < 5))
    tops = [dot(state[:, 128:], pick_top) for state in states]
    best = functools.reduce(jnp.maximum, tops)
    factors = [jnp.exp(top - best) for top in tops]
    total = sum(dot(state[:, 128:], pick_total) * factor for state, factor in zip(states, factors))
    acc = sum(state.astype(F32) * factor for state, factor in zip(states, factors))
    return best, total, acc


def pair_kernel(*refs):
    states, outs = refs[:-4], refs[-4:]
    best, total, acc = merged([state[...] for state in states])
    rows = acc.shape[0]
    lane = iota((rows, 128), 1)
    part, slot = lane >> 3, lane & 7
    stats = jnp.zeros((rows, 128), F32)
    for head, column in enumerate((128, 0, HD)):
        stats = jnp.where((slot == head) & (part < 3), best[:, column : column + 1], stats)
        stats = jnp.where((slot == head) & (part >= 3), total[:, column : column + 1], stats)
    left = acc[:, :128].astype(BF)
    right = jnp.where(lane < HD, split(stats, part), acc[:, 128:]).astype(BF)
    count = rows // 4
    for k, out in enumerate(outs):
        out[:, :128] = left[k * count : (k + 1) * count]
        out[:, 128:] = right[k * count : (k + 1) * count]


def finish_kernel(mine_ref, core_ref, far_ref, far_core_ref, coarse_ref, mid_ref, w_cout_ref, w_up_ref, out_ref):
    core = lax.axis_index("core")
    half = w_cout_ref.shape[0] // 2
    attended = jnp.zeros(coarse_ref.shape, F32)
    for heads, states in ((core, (mine_ref, far_ref)), (1 - core, (core_ref, far_core_ref))):
        _, total, acc = merged([state[...] for state in states])
        value = (acc / total).astype(BF)
        value = jnp.concatenate([value[:, 3 * HD :], value[:, : 2 * HD]], axis=1)
        attended += dot(value, w_cout_ref[pl.ds(pl.multiple_of(heads * half, half), half), :])
    coarse_mid = (coarse_ref[...].astype(F32) + attended).astype(BF)
    upper = dot(coarse_mid, w_up_ref[...])
    upper = jnp.concatenate([upper[:, part * D : (part + 1) * D] for part in range(4)], axis=0)
    fine = (mid_ref[...].astype(F32) + upper).astype(BF)
    out_ref[...] = dot(one_hot(natural_of(iota((N, N), 1)) == iota((N, N), 0)), fine).astype(BF)


def call(kernel, outs, scratch=(), smem=0, micros=0, short=False):
    vmem = pl.BlockSpec(memory_space=pltpu.VMEM)
    cost = pl.CostEstimate(flops=micros * 10**9, transcendentals=0, bytes_accessed=micros << 21) if micros else None
    if short:
        cost = pl.CostEstimate(flops=1000, transcendentals=0, bytes_accessed=1000)

    def run(*args):
        return pl.pallas_call(
            kernel,
            out_shape=[jax.ShapeDtypeStruct(shape, BF if kind is None else kind) for shape, kind in outs],
            in_specs=[pl.BlockSpec(memory_space=pltpu.SMEM)] * smem + [vmem] * (len(args) - smem),
            out_specs=[vmem] * len(outs),
            scratch_shapes=list(scratch),
            cost_estimate=cost,
            compiler_params=pltpu.CompilerParams(vmem_limit_bytes=40 * 1024 * 1024),
        )(*args)

    return run


def permuted(value, target):
    pairs = []
    for at in itertools.product(*(range(size) for size in SIZES)):
        to = target(*at)
        if to is not None:
            pairs.append((int(np.ravel_multi_index(at, SIZES)), int(np.ravel_multi_index(to, SIZES))))
    return lax.ppermute(value, AXES, pairs)


def partner(index, far):
    other = index ^ 1 if not far else (index + 1 if index % 2 else index - 1)
    return other if 0 <= other < 16 else None


def row_partner(far):
    def target(zl, y, zh, x, core):
        to = partner(zl * 4 + y, far)
        return None if to is None else (to // 4, to % 4, zh, x, core)

    return target


def col_partner(far):
    def target(zl, y, zh, x, core):
        to = partner(zh * 8 + x * 2 + core, far)
        return None if to is None else (zl, y, to // 8, to // 2 % 4, to % 2)

    return target


def along_z(step):
    def target(zl, y, zh, x, core):
        z = (zh * 4 + zl) ^ step
        return (z % 4, y, z // 4, x, core)

    return target


def other_core(zl, y, zh, x, core):
    return (zl, y, zh, x, 1 - core)


def far_chip(zl, y, zh, x, core):
    return (zl ^ 1, y, zh, x, core)


def far_other(zl, y, zh, x, core):
    return (zl ^ 1, y, zh, x, 1 - core)


def per_device(tokens, stale_kv, timestep, w_time, w_qkv, w_out, w_merge, w_cqkv, w_cout, w_up):
    width, coarse_width = w_cout.shape
    count = N // 4
    band = ((3, SIDE, 2 * D), None)
    row_near, row_far = call(rows_kernel, [band, band], micros=4)(stale_kv)
    row_near = permuted(row_near, row_partner(False))
    row_far = permuted(row_far, row_partner(True))
    query, kv, fresh_kv, gate, mine = call(
        project_kernel,
        [((N, D), None), ((N, 2 * D), None), ((N, 2 * D), None), ((8, D), F32), ((N, D), None)],
        smem=1,
        micros=8,
    )(timestep, tokens.reshape(N, D), w_time, w_qkv)
    col_near, col_far = call(columns_kernel, [((EDGE, 2 * D), None)] * 2, micros=2)(stale_kv, row_near, row_far)
    col_near = permuted(col_near, col_partner(False))
    col_far = permuted(col_far, col_partner(True))
    mid, coarse, cq, other, ckv = call(
        fine_kernel,
        [((N, D), None), ((count, coarse_width), None), ((count, 256), None), ((count, 256), None), ((32, count, width), None)],
        scratch=[pltpu.VMEM((N, 2 * D), BF)],
        micros=3,
    )(query, kv, gate, mine, row_near, row_far, col_near, col_far, w_out, w_merge, w_cqkv)
    ckv = lax.all_to_all(ckv, ("y", "x", "core"), 0, 0)
    other = permuted(other, other_core)
    (block,) = call(chip_kernel, [((2 * count, 256), None)])(cq, other)
    block = jnp.concatenate([block, permuted(block, along_z(1))], axis=0)
    blocks = {step: permuted(block, along_z(step)) for step in (4, 2, 6)}
    keys_values = ckv.reshape(32 * count, width)
    states = []
    before = []
    for step in (4, 2, 6, 0):
        early = before + (states[:1] if step == 0 else [])
        (state,) = call(coarse_kernel, [((4 * count, 256), None)], short=True)(keys_values, blocks.get(step, block), *early)
        before = [state]
        states.append(permuted(state, along_z(step)) if step else state)
    mine, core, far, far_core = call(pair_kernel, [((count, 256), None)] * 4)(*states)
    far, core, far_core = permuted(far, far_chip), permuted(core, other_core), permuted(far_core, far_other)
    (fine_out,) = call(finish_kernel, [((N, D), None)], micros=2)(mine, core, far, far_core, coarse, mid, w_cout, w_up)
    return (fine_out.reshape(SIDE, SIDE, D), fresh_kv.reshape(SIDE, SIDE, 2 * D))


def solution(mesh):
    fine = Mesh(mesh.devices.reshape(SIZES), AXES)
    tiled = P(("zl", "y"), ("zh", "x", "core"), None)
    return jax.shard_map(
        per_device,
        mesh=fine,
        in_specs=(tiled, tiled) + (P(),) * 8,
        out_specs=(tiled, tiled),
        check_vma=False,
    )
```

```python
import functools
import itertools
import math

import jax
import jax.numpy as jnp
import numpy as np
from jax import lax
from jax.experimental import pallas as pl
from jax.experimental.pallas import tpu as pltpu
from jax.sharding import Mesh
from jax.sharding import PartitionSpec as P

HD = 64
SIDE = 16
N = SIDE * SIDE
D = 256
BAND = 3 * SIDE
EDGE = 80
BF = jnp.bfloat16
F32 = jnp.float32
AXES = ("zl", "y", "zh", "x", "core")
SIZES = (4, 4, 2, 4, 2)


def dot(a, b):
    return lax.dot_general(a, b, (((1,), (0,)), ((), ())), preferred_element_type=F32)


def dot_t(a, b):
    return lax.dot_general(a, b, (((1,), (1,)), ((), ())), preferred_element_type=F32)


def one_hot(condition):
    return condition.astype(F32).astype(BF)


def iota(shape, dim):
    return lax.broadcasted_iota(jnp.int32, shape, dim)


def tile_row():
    return lax.axis_index("zl") * 4 + lax.axis_index("y")


def tile_col():
    return lax.axis_index("zh") * 8 + lax.axis_index("x") * 2 + lax.axis_index("core")


def third(n):
    return (n * 171) >> 9


def layer_norm(values):
    values = values.astype(F32)
    mean = jnp.mean(values, axis=-1, keepdims=True)
    centred = values - mean
    var = jnp.mean(centred * centred, axis=-1, keepdims=True)
    return centred * lax.rsqrt(var + 1e-06)


def natural_of(m):
    a, b, r, c = m >> 7, (m >> 6) & 1, (m >> 3) & 7, m & 7
    return (2 * r + a) * SIDE + 2 * c + b


def rows_kernel(stale_ref, near_ref, far_ref):
    odd = tile_row() % 2
    near_ref[...] = stale_ref[pl.ds((1 - odd) * 13, 3)]
    far_ref[...] = stale_ref[pl.ds(odd * 13, 3)]


def columns_kernel(stale_ref, row_near_ref, row_far_ref, near_ref, far_ref):
    odd = tile_col() % 2
    stale = stale_ref[...].reshape(N, 2 * D)
    row_near = row_near_ref[...].reshape(BAND, 2 * D)
    row_far = row_far_ref[...].reshape(BAND, 2 * D)
    for out, first in ((near_ref, (1 - odd) * 13), (far_ref, odd * 13)):
        take, source = iota((BAND, N), 0), iota((BAND, N), 1)
        i = third(take)
        out[:BAND, :] = dot(one_hot(source == i * SIDE + first + take - 3 * i), stale).astype(BF)
        take, source = iota((SIDE, BAND), 0), iota((SIDE, BAND), 1)
        i = third(take)
        corner = one_hot((source == i * SIDE + first + take - 3 * i) & (take < 9))
        out[BAND : BAND + SIDE, :] = dot(corner, row_near).astype(BF)
        out[BAND + SIDE :, :] = dot(corner, row_far).astype(BF)


def project_kernel(time_ref, tokens_ref, w_time_ref, w_qkv_ref, q_ref, kv_ref, kv_out_ref, gate_ref, mine_ref):
    half = D // 2
    index = iota((8, half), 1).astype(F32)
    angle = time_ref[0].astype(F32) * jnp.exp(-math.log(10000.0) * index * 2.0 / D)
    emb = jnp.concatenate([jnp.cos(angle), jnp.sin(angle)], axis=1)
    act = (emb / (1.0 + jnp.exp(-emb))).astype(BF)
    mod = dot(act, w_time_ref[...])
    gate_ref[...] = mod[:, 2 * D :]
    regroup = one_hot(natural_of(iota((N, N), 0)) == iota((N, N), 1))
    tokens = tokens_ref[...]
    mine_ref[...] = dot(regroup, tokens).astype(BF)
    normed = (layer_norm(tokens) * (1.0 + mod[0:1, D : 2 * D]) + mod[0:1, :D]).astype(BF)
    kv = dot(normed, w_qkv_ref[:, D:]).astype(BF)
    kv_ref[...] = kv
    kv_out_ref[...] = kv
    q_ref[...] = dot(dot(regroup, normed).astype(BF), w_qkv_ref[:, :D]).astype(BF)


def fine_kernel(q_ref, kv_ref, gate_ref, mine_ref, row_near_ref, row_far_ref, col_near_ref, col_far_ref,
                w_out_ref, w_merge_ref, w_cqkv_ref,
                mid_ref, coarse_ref, mine_out_ref, other_ref, ckv_ref, halo):
    halo[:BAND, :] = row_near_ref[...].reshape(BAND, 2 * D)
    halo[BAND : 2 * BAND, :] = row_far_ref[...].reshape(BAND, 2 * D)
    halo[2 * BAND : 2 * BAND + EDGE, :] = col_near_ref[...]
    halo[2 * BAND + EDGE :, :] = col_far_ref[...]

    row, col = tile_row(), tile_col()
    row_odd, col_odd = row % 2, col % 2

    def after(odd):
        return (1 - odd) * SIDE - 3 * odd

    near_i, far_i = after(row_odd), after(1 - row_odd)
    near_j, far_j = after(col_odd), after(1 - col_odd)
    k = iota((1, N), 1)
    own_i, own_j = k >> 4, k & 15
    edge = jnp.where(k >= 2 * BAND + EDGE, k - 2 * BAND - EDGE, k - 2 * BAND)
    edge = jnp.maximum(edge, 0)
    cut = jnp.where(edge < BAND, edge, (edge - BAND) & 15)
    step = third(cut)
    side_i = jnp.where(edge < BAND, step, jnp.where(edge < BAND + SIDE, near_i, far_i) + step)
    side_j = jnp.where(k >= 2 * BAND + EDGE, far_j, near_j) + cut - 3 * step
    side_i = jnp.where((edge >= BAND) & (cut >= 9), -1000, side_i)
    band = jnp.where(k >= BAND, k - BAND, k)
    band_i = jnp.where(k >= BAND, far_i, near_i) + (band >> 4)
    halo_i = jnp.where(k < 2 * BAND, band_i, side_i)
    halo_j = jnp.where(k < 2 * BAND, band & 15, side_j)
    ki = jnp.concatenate([own_i, halo_i], axis=1)
    kj = jnp.concatenate([own_j, halo_j], axis=1)
    at_i, at_j = ki + row * SIDE, kj + col * SIDE
    in_image = (at_i >= 0) & (at_i < 16 * SIDE) & (at_j >= 0) & (at_j < 16 * SIDE)
    ki = jnp.where(in_image, ki, -1000)
    natural = natural_of(iota((N, 1), 0))
    near = (jnp.abs((natural >> 4) - ki) <= 3) & (jnp.abs((natural & 15) - kj) <= 3)

    lane = iota((N, 128), 1)
    attn = []
    for pair in range(D // 128):
        cols = slice(pair * 128, pair * 128 + 128)
        vcols = slice(D + pair * 128, D + pair * 128 + 128)
        q2 = q_ref[:, cols]
        halves = []
        for which in range(2):
            q1 = jnp.where((lane < HD) if which == 0 else (lane >= HD), q2, jnp.zeros_like(q2))
            score = jnp.concatenate([dot_t(q1, kv_ref[:, cols]), dot_t(q1, halo[:, cols])], axis=1)
            score = jnp.where(near, score * (1.0 / math.sqrt(HD)), -1e30)
            expo = jnp.exp(score - jnp.max(score, axis=1, keepdims=True))
            total = jnp.sum(expo, axis=1, keepdims=True)
            weights = expo.astype(BF)
            acc = dot(weights[:, :N], kv_ref[:, vcols]) + dot(weights[:, N:], halo[:, vcols])
            halves.append(acc / total)
        attn.append(jnp.where(lane < HD, halves[0], halves[1]).astype(BF))
    attn = jnp.concatenate(attn, axis=1)
    mid = (mine_ref[...].astype(F32) + gate_ref[0:1, :] * dot(attn, w_out_ref[...])).astype(BF)
    mid_ref[...] = mid
    quarter = N // 4
    coarse = sum(
        dot(mid[part * quarter : (part + 1) * quarter, :], w_merge_ref[part * D : (part + 1) * D, :])
        for part in range(4)
    ).astype(BF)
    coarse_ref[...] = coarse
    cqkv = dot(layer_norm(coarse).astype(BF), w_cqkv_ref[...]).astype(BF)
    width = w_cqkv_ref.shape[1] // 3
    half = width // 2
    halves = []
    for which in range(2):
        starts = [part * width + which * half for part in range(3)]
        halves.append([cqkv[:, start : start + half] for start in starts])
    core = lax.axis_index("core")
    pad = jnp.zeros((quarter, HD), BF)
    queries = [jnp.concatenate([q * BF(1.0 / math.sqrt(HD)), pad], axis=1) for q, _, _ in halves]
    mine_out_ref[...] = jnp.where(core == 0, queries[0], queries[1])
    other_ref[...] = jnp.where(core == 0, queries[1], queries[0])
    for which in range(2):
        ckv_ref[which] = jnp.concatenate(halves[which][1:], axis=1)
    for block in range(2, ckv_ref.shape[0]):
        ckv_ref[block] = ckv_ref[block % 2]


def chip_kernel(mine_ref, other_ref, out_ref):
    count = mine_ref.shape[0]
    out_ref[:count, :] = mine_ref[...]
    out_ref[count:, :] = other_ref[...]


def coarse_kernel(kv_ref, queries_ref, *rest):
    out_ref = rest[-1]
    blocks = 2
    rows = queries_ref.shape[0] // blocks
    lane = iota((rows, 128), 1)
    low = lane < HD
    part, slot = lane >> 3, lane & 7
    ones = jnp.ones((kv_ref.shape[0], 128), BF)
    for block in range(blocks):
        here = slice(block * rows, (block + 1) * rows)
        q2, q3 = queries_ref[here, :128], queries_ref[here, 128:]
        zero = jnp.zeros_like(q2)
        pair = jnp.concatenate([jnp.where(low, q2, zero), jnp.where(low, zero, q2)], axis=0)
        score = dot_t(pair, kv_ref[:, :128])
        scores = [score[:rows], score[rows:], dot_t(q3, kv_ref[:, 128:256])]
        tops = [jnp.max(score, axis=1, keepdims=True) for score in scores]
        weights = [jnp.exp(score - top).astype(BF) for score, top in zip(scores, tops)]
        first = dot(weights[0], jnp.concatenate([kv_ref[:, 128:256], ones], axis=1))
        pair = dot(jnp.concatenate(weights[1:], axis=0), jnp.concatenate([kv_ref[:, 256:], ones], axis=1))
        sums = [first, pair[:rows], pair[rows:]]
        stats = jnp.zeros((rows, 128), F32)
        for head in range(3):
            stats = jnp.where((slot == head) & (part < 3), tops[head], stats)
            stats = jnp.where((slot == head) & (part >= 3), sums[head][:, 128:], stats)
        out_ref[here, :128] = jnp.where(low, sums[1][:, :128], sums[2][:, :128]).astype(BF)
        out_ref[here, 128:] = jnp.where(low, split(stats, part), first[:, :128]).astype(BF)


def split(stats, part):
    high = stats.astype(BF).astype(F32)
    middle = (stats - high).astype(BF).astype(F32)
    last = stats - high - middle
    return jnp.where((part == 0) | (part == 3), high, jnp.where((part == 1) | (part == 4), middle, last))


def merged(states):
    row, column = iota((128, 256), 0), iota((128, 256), 1)
    head = jnp.where(column < HD, 1, jnp.where(column < 2 * HD, 2, 0))
    part, slot = row >> 3, row & 7
    pick_top = one_hot((slot == head) & (part < 3))
    pick_total = one_hot((slot == head) & (part >= 3) & (part < 5))
    tops = [dot(state[:, 128:], pick_top) for state in states]
    best = functools.reduce(jnp.maximum, tops)
    factors = [jnp.exp(top - best) for top in tops]
    total = sum(dot(state[:, 128:], pick_total) * factor for state, factor in zip(states, factors))
    acc = sum(state.astype(F32) * factor for state, factor in zip(states, factors))
    return best, total, acc


def pair_kernel(*refs):
    states, outs = refs[:-4], refs[-4:]
    best, total, acc = merged([state[...] for state in states])
    rows = acc.shape[0]
    lane = iota((rows, 128), 1)
    part, slot = lane >> 3, lane & 7
    stats = jnp.zeros((rows, 128), F32)
    for head, column in enumerate((128, 0, HD)):
        stats = jnp.where((slot == head) & (part < 3), best[:, column : column + 1], stats)
        stats = jnp.where((slot == head) & (part >= 3), total[:, column : column + 1], stats)
    left = acc[:, :128].astype(BF)
    right = jnp.where(lane < HD, split(stats, part), acc[:, 128:]).astype(BF)
    count = rows // 4
    for k, out in enumerate(outs):
        out[:, :128] = left[k * count : (k + 1) * count]
        out[:, 128:] = right[k * count : (k + 1) * count]


def finish_kernel(mine_ref, core_ref, far_ref, far_core_ref, coarse_ref, mid_ref, w_cout_ref, w_up_ref, out_ref):
    core = lax.axis_index("core")
    half = w_cout_ref.shape[0] // 2
    attended = jnp.zeros(coarse_ref.shape, F32)
    for heads, states in ((core, (mine_ref, far_ref)), (1 - core, (core_ref, far_core_ref))):
        _, total, acc = merged([state[...] for state in states])
        value = (acc / total).astype(BF)
        value = jnp.concatenate([value[:, 3 * HD :], value[:, : 2 * HD]], axis=1)
        attended += dot(value, w_cout_ref[pl.ds(pl.multiple_of(heads * half, half), half), :])
    coarse_mid = (coarse_ref[...].astype(F32) + attended).astype(BF)
    upper = dot(coarse_mid, w_up_ref[...])
    upper = jnp.concatenate([upper[:, part * D : (part + 1) * D] for part in range(4)], axis=0)
    fine = (mid_ref[...].astype(F32) + upper).astype(BF)
    out_ref[...] = dot(one_hot(natural_of(iota((N, N), 1)) == iota((N, N), 0)), fine).astype(BF)


def call(kernel, outs, scratch=(), smem=0, micros=0, short=False):
    vmem = pl.BlockSpec(memory_space=pltpu.VMEM)
    cost = pl.CostEstimate(flops=micros * 10**9, transcendentals=0, bytes_accessed=micros << 21) if micros else None
    if short:
        cost = pl.CostEstimate(flops=1000, transcendentals=0, bytes_accessed=1000)

    def run(*args):
        return pl.pallas_call(
            kernel,
            out_shape=[jax.ShapeDtypeStruct(shape, BF if kind is None else kind) for shape, kind in outs],
            in_specs=[pl.BlockSpec(memory_space=pltpu.SMEM)] * smem + [vmem] * (len(args) - smem),
            out_specs=[vmem] * len(outs),
            scratch_shapes=list(scratch),
            cost_estimate=cost,
            compiler_params=pltpu.CompilerParams(vmem_limit_bytes=40 * 1024 * 1024),
        )(*args)

    return run


def permuted(value, target):
    pairs = []
    for at in itertools.product(*(range(size) for size in SIZES)):
        to = target(*at)
        if to is not None:
            pairs.append((int(np.ravel_multi_index(at, SIZES)), int(np.ravel_multi_index(to, SIZES))))
    return lax.ppermute(value, AXES, pairs)


def partner(index, far):
    other = index ^ 1 if not far else (index + 1 if index % 2 else index - 1)
    return other if 0 <= other < 16 else None


def row_partner(far):
    def target(zl, y, zh, x, core):
        to = partner(zl * 4 + y, far)
        return None if to is None else (to // 4, to % 4, zh, x, core)

    return target


def col_partner(far):
    def target(zl, y, zh, x, core):
        to = partner(zh * 8 + x * 2 + core, far)
        return None if to is None else (zl, y, to // 8, to // 2 % 4, to % 2)

    return target


def along_z(step):
    def target(zl, y, zh, x, core):
        z = (zh * 4 + zl) ^ step
        return (z % 4, y, z // 4, x, core)

    return target


def other_core(zl, y, zh, x, core):
    return (zl, y, zh, x, 1 - core)


def far_chip(zl, y, zh, x, core):
    return (zl ^ 1, y, zh, x, core)


def far_other(zl, y, zh, x, core):
    return (zl ^ 1, y, zh, x, 1 - core)


def per_device(tokens, stale_kv, timestep, w_time, w_qkv, w_out, w_merge, w_cqkv, w_cout, w_up):
    width, coarse_width = w_cout.shape
    count = N // 4
    band = ((3, SIDE, 2 * D), None)
    row_near, row_far = call(rows_kernel, [band, band], micros=4)(stale_kv)
    row_near = permuted(row_near, row_partner(False))
    row_far = permuted(row_far, row_partner(True))
    query, kv, fresh_kv, gate, mine = call(
        project_kernel,
        [((N, D), None), ((N, 2 * D), None), ((N, 2 * D), None), ((8, D), F32), ((N, D), None)],
        smem=1,
        micros=8,
    )(timestep, tokens.reshape(N, D), w_time, w_qkv)
    col_near, col_far = call(columns_kernel, [((EDGE, 2 * D), None)] * 2, micros=2)(stale_kv, row_near, row_far)
    col_near = permuted(col_near, col_partner(False))
    col_far = permuted(col_far, col_partner(True))
    mid, coarse, cq, other, ckv = call(
        fine_kernel,
        [((N, D), None), ((count, coarse_width), None), ((count, 256), None), ((count, 256), None), ((32, count, width), None)],
        scratch=[pltpu.VMEM((N, 2 * D), BF)],
        micros=3,
    )(query, kv, gate, mine, row_near, row_far, col_near, col_far, w_out, w_merge, w_cqkv)
    ckv = lax.all_to_all(ckv, ("y", "x", "core"), 0, 0)
    other = permuted(other, other_core)
    (block,) = call(chip_kernel, [((2 * count, 256), None)])(cq, other)
    block = jnp.concatenate([block, permuted(block, along_z(1))], axis=0)
    blocks = {step: permuted(block, along_z(step)) for step in (4, 2, 6)}
    keys_values = ckv.reshape(32 * count, width)
    states = []
    before = []
    for step in (4, 2, 6, 0):
        early = before + (states[:1] if step == 0 else [])
        (state,) = call(coarse_kernel, [((4 * count, 256), None)], short=True)(keys_values, blocks.get(step, block), *early)
        before = [state]
        states.append(permuted(state, along_z(step)) if step else state)
    mine, core, far, far_core = call(pair_kernel, [((count, 256), None)] * 4)(*states)
    far, core, far_core = permuted(far, far_chip), permuted(core, other_core), permuted(far_core, far_other)
    (fine_out,) = call(finish_kernel, [((N, D), None)], micros=2)(mine, core, far, far_core, coarse, mid, w_cout, w_up)
    return (fine_out.reshape(SIDE, SIDE, D), fresh_kv.reshape(SIDE, SIDE, 2 * D))


def solution(mesh):
    fine = Mesh(mesh.devices.reshape(SIZES), AXES)
    tiled = P(("zl", "y"), ("zh", "x", "core"), None)
    return jax.shard_map(
        per_device,
        mesh=fine,
        in_specs=(tiled, tiled) + (P(),) * 8,
        out_specs=(tiled, tiled),
        check_vma=False,
    )
```

```python
import functools
import itertools
import math

import jax
import jax.numpy as jnp
import numpy as np
from jax import lax
from jax.experimental import pallas as pl
from jax.experimental.pallas import tpu as pltpu
from jax.sharding import Mesh
from jax.sharding import PartitionSpec as P

HD = 64
SIDE = 16
N = SIDE * SIDE
D = 256
BAND = 3 * SIDE
EDGE = 80
BF = jnp.bfloat16
F32 = jnp.float32
AXES = ("zl", "y", "zh", "x", "core")
SIZES = (4, 4, 2, 4, 2)


def dot(a, b):
    return lax.dot_general(a, b, (((1,), (0,)), ((), ())), preferred_element_type=F32)


def dot_t(a, b):
    return lax.dot_general(a, b, (((1,), (1,)), ((), ())), preferred_element_type=F32)


def one_hot(condition):
    return condition.astype(F32).astype(BF)


def iota(shape, dim):
    return lax.broadcasted_iota(jnp.int32, shape, dim)


def tile_row():
    return lax.axis_index("zl") * 4 + lax.axis_index("y")


def tile_col():
    return lax.axis_index("zh") * 8 + lax.axis_index("x") * 2 + lax.axis_index("core")


def third(n):
    return (n * 171) >> 9


def layer_norm(values):
    values = values.astype(F32)
    mean = jnp.mean(values, axis=-1, keepdims=True)
    centred = values - mean
    var = jnp.mean(centred * centred, axis=-1, keepdims=True)
    return centred * lax.rsqrt(var + 1e-06)


def natural_of(m):
    a, b, r, c = m >> 7, (m >> 6) & 1, (m >> 3) & 7, m & 7
    return (2 * r + a) * SIDE + 2 * c + b


def rows_kernel(stale_ref, near_ref, far_ref):
    odd = tile_row() % 2
    near_ref[...] = stale_ref[pl.ds((1 - odd) * 13, 3)]
    far_ref[...] = stale_ref[pl.ds(odd * 13, 3)]


def columns_kernel(stale_ref, row_near_ref, row_far_ref, near_ref, far_ref):
    odd = tile_col() % 2
    stale = stale_ref[...].reshape(N, 2 * D)
    row_near = row_near_ref[...].reshape(BAND, 2 * D)
    row_far = row_far_ref[...].reshape(BAND, 2 * D)
    for out, first in ((near_ref, (1 - odd) * 13), (far_ref, odd * 13)):
        take, source = iota((BAND, N), 0), iota((BAND, N), 1)
        i = third(take)
        out[:BAND, :] = dot(one_hot(source == i * SIDE + first + take - 3 * i), stale).astype(BF)
        take, source = iota((SIDE, BAND), 0), iota((SIDE, BAND), 1)
        i = third(take)
        corner = one_hot((source == i * SIDE + first + take - 3 * i) & (take < 9))
        out[BAND : BAND + SIDE, :] = dot(corner, row_near).astype(BF)
        out[BAND + SIDE :, :] = dot(corner, row_far).astype(BF)


def project_kernel(time_ref, tokens_ref, w_time_ref, w_qkv_ref, q_ref, kv_ref, kv_out_ref, gate_ref, mine_ref):
    half = D // 2
    index = iota((8, half), 1).astype(F32)
    angle = time_ref[0].astype(F32) * jnp.exp(-math.log(10000.0) * index * 2.0 / D)
    emb = jnp.concatenate([jnp.cos(angle), jnp.sin(angle)], axis=1)
    act = (emb / (1.0 + jnp.exp(-emb))).astype(BF)
    mod = dot(act, w_time_ref[...])
    gate_ref[...] = mod[:, 2 * D :]
    regroup = one_hot(natural_of(iota((N, N), 0)) == iota((N, N), 1))
    tokens = tokens_ref[...]
    mine_ref[...] = dot(regroup, tokens).astype(BF)
    normed = (layer_norm(tokens) * (1.0 + mod[0:1, D : 2 * D]) + mod[0:1, :D]).astype(BF)
    kv = dot(normed, w_qkv_ref[:, D:]).astype(BF)
    kv_ref[...] = kv
    kv_out_ref[...] = kv
    q_ref[...] = dot(dot(regroup, normed).astype(BF), w_qkv_ref[:, :D]).astype(BF)


def fine_kernel(q_ref, kv_ref, gate_ref, mine_ref, row_near_ref, row_far_ref, col_near_ref, col_far_ref,
                w_out_ref, w_merge_ref, w_cqkv_ref,
                mid_ref, coarse_ref, mine_out_ref, other_ref, ckv_ref, halo, sets, sems):
    halo[:BAND, :] = row_near_ref[...].reshape(BAND, 2 * D)
    halo[BAND : 2 * BAND, :] = row_far_ref[...].reshape(BAND, 2 * D)
    halo[2 * BAND : 2 * BAND + EDGE, :] = col_near_ref[...]
    halo[2 * BAND + EDGE :, :] = col_far_ref[...]

    row, col = tile_row(), tile_col()
    row_odd, col_odd = row % 2, col % 2

    def after(odd):
        return (1 - odd) * SIDE - 3 * odd

    near_i, far_i = after(row_odd), after(1 - row_odd)
    near_j, far_j = after(col_odd), after(1 - col_odd)
    k = iota((1, N), 1)
    own_i, own_j = k >> 4, k & 15
    edge = jnp.where(k >= 2 * BAND + EDGE, k - 2 * BAND - EDGE, k - 2 * BAND)
    edge = jnp.maximum(edge, 0)
    cut = jnp.where(edge < BAND, edge, (edge - BAND) & 15)
    step = third(cut)
    side_i = jnp.where(edge < BAND, step, jnp.where(edge < BAND + SIDE, near_i, far_i) + step)
    side_j = jnp.where(k >= 2 * BAND + EDGE, far_j, near_j) + cut - 3 * step
    side_i = jnp.where((edge >= BAND) & (cut >= 9), -1000, side_i)
    band = jnp.where(k >= BAND, k - BAND, k)
    band_i = jnp.where(k >= BAND, far_i, near_i) + (band >> 4)
    halo_i = jnp.where(k < 2 * BAND, band_i, side_i)
    halo_j = jnp.where(k < 2 * BAND, band & 15, side_j)
    ki = jnp.concatenate([own_i, halo_i], axis=1)
    kj = jnp.concatenate([own_j, halo_j], axis=1)
    at_i, at_j = ki + row * SIDE, kj + col * SIDE
    in_image = (at_i >= 0) & (at_i < 16 * SIDE) & (at_j >= 0) & (at_j < 16 * SIDE)
    ki = jnp.where(in_image, ki, -1000)
    natural = natural_of(iota((N, 1), 0))
    near = (jnp.abs((natural >> 4) - ki) <= 3) & (jnp.abs((natural & 15) - kj) <= 3)

    lane = iota((N, 128), 1)
    attn = []
    for pair in range(D // 128):
        cols = slice(pair * 128, pair * 128 + 128)
        vcols = slice(D + pair * 128, D + pair * 128 + 128)
        q2 = q_ref[:, cols]
        halves = []
        for which in range(2):
            q1 = jnp.where((lane < HD) if which == 0 else (lane >= HD), q2, jnp.zeros_like(q2))
            score = jnp.concatenate([dot_t(q1, kv_ref[:, cols]), dot_t(q1, halo[:, cols])], axis=1)
            score = jnp.where(near, score * (1.0 / math.sqrt(HD)), -1e30)
            expo = jnp.exp(score - jnp.max(score, axis=1, keepdims=True))
            total = jnp.sum(expo, axis=1, keepdims=True)
            weights = expo.astype(BF)
            acc = dot(weights[:, :N], kv_ref[:, vcols]) + dot(weights[:, N:], halo[:, vcols])
            halves.append(acc / total)
        attn.append(jnp.where(lane < HD, halves[0], halves[1]).astype(BF))
    attn = jnp.concatenate(attn, axis=1)
    mid = (mine_ref[...].astype(F32) + gate_ref[0:1, :] * dot(attn, w_out_ref[...])).astype(BF)
    mid_ref[...] = mid
    quarter = N // 4
    coarse = sum(
        dot(mid[part * quarter : (part + 1) * quarter, :], w_merge_ref[part * D : (part + 1) * D, :])
        for part in range(4)
    ).astype(BF)
    coarse_ref[...] = coarse
    cqkv = dot(layer_norm(coarse).astype(BF), w_cqkv_ref[...]).astype(BF)
    width = w_cqkv_ref.shape[1] // 3
    half = width // 2
    halves = []
    for which in range(2):
        starts = [part * width + which * half for part in range(3)]
        halves.append([cqkv[:, start : start + half] for start in starts])
    for which in range(2):
        sets[which] = jnp.concatenate(halves[which][1:], axis=1)
    copies = [pltpu.make_async_copy(sets, ckv_ref.at[chip], sems.at[chip]) for chip in range(ckv_ref.shape[0])]
    for copy in copies:
        copy.start()
    core = lax.axis_index("core")
    pad = jnp.zeros((quarter, HD), BF)
    queries = [jnp.concatenate([q * BF(1.0 / math.sqrt(HD)), pad], axis=1) for q, _, _ in halves]
    mine_out_ref[...] = jnp.where(core == 0, queries[0], queries[1])
    other_ref[...] = jnp.where(core == 0, queries[1], queries[0])
    for copy in copies:
        copy.wait()


def chip_kernel(mine_ref, other_ref, out_ref):
    count = mine_ref.shape[0]
    out_ref[:count, :] = mine_ref[...]
    out_ref[count:, :] = other_ref[...]


def coarse_kernel(kv_ref, queries_ref, *rest):
    out_ref = rest[-1]
    blocks = 2
    rows = queries_ref.shape[0] // blocks
    lane = iota((rows, 128), 1)
    low = lane < HD
    part, slot = lane >> 3, lane & 7
    ones = jnp.ones((kv_ref.shape[0], 128), BF)
    for block in range(blocks):
        here = slice(block * rows, (block + 1) * rows)
        q2, q3 = queries_ref[here, :128], queries_ref[here, 128:]
        zero = jnp.zeros_like(q2)
        pair = jnp.concatenate([jnp.where(low, q2, zero), jnp.where(low, zero, q2)], axis=0)
        score = dot_t(pair, kv_ref[:, :128])
        scores = [score[:rows], score[rows:], dot_t(q3, kv_ref[:, 128:256])]
        tops = [jnp.max(score, axis=1, keepdims=True) for score in scores]
        weights = [jnp.exp(score - top).astype(BF) for score, top in zip(scores, tops)]
        first = dot(weights[0], jnp.concatenate([kv_ref[:, 128:256], ones], axis=1))
        pair = dot(jnp.concatenate(weights[1:], axis=0), jnp.concatenate([kv_ref[:, 256:], ones], axis=1))
        sums = [first, pair[:rows], pair[rows:]]
        stats = jnp.zeros((rows, 128), F32)
        for head in range(3):
            stats = jnp.where((slot == head) & (part < 3), tops[head], stats)
            stats = jnp.where((slot == head) & (part >= 3), sums[head][:, 128:], stats)
        out_ref[here, :128] = jnp.where(low, sums[1][:, :128], sums[2][:, :128]).astype(BF)
        out_ref[here, 128:] = jnp.where(low, split(stats, part), first[:, :128]).astype(BF)


def split(stats, part):
    high = stats.astype(BF).astype(F32)
    middle = (stats - high).astype(BF).astype(F32)
    last = stats - high - middle
    return jnp.where((part == 0) | (part == 3), high, jnp.where((part == 1) | (part == 4), middle, last))


def merged(states):
    row, column = iota((128, 256), 0), iota((128, 256), 1)
    head = jnp.where(column < HD, 1, jnp.where(column < 2 * HD, 2, 0))
    part, slot = row >> 3, row & 7
    pick_top = one_hot((slot == head) & (part < 3))
    pick_total = one_hot((slot == head) & (part >= 3) & (part < 5))
    tops = [dot(state[:, 128:], pick_top) for state in states]
    best = functools.reduce(jnp.maximum, tops)
    factors = [jnp.exp(top - best) for top in tops]
    total = sum(dot(state[:, 128:], pick_total) * factor for state, factor in zip(states, factors))
    acc = sum(state.astype(F32) * factor for state, factor in zip(states, factors))
    return best, total, acc


def pair_kernel(*refs):
    states, outs = refs[:-4], refs[-4:]
    best, total, acc = merged([state[...] for state in states])
    rows = acc.shape[0]
    lane = iota((rows, 128), 1)
    part, slot = lane >> 3, lane & 7
    stats = jnp.zeros((rows, 128), F32)
    for head, column in enumerate((128, 0, HD)):
        stats = jnp.where((slot == head) & (part < 3), best[:, column : column + 1], stats)
        stats = jnp.where((slot == head) & (part >= 3), total[:, column : column + 1], stats)
    left = acc[:, :128].astype(BF)
    right = jnp.where(lane < HD, split(stats, part), acc[:, 128:]).astype(BF)
    count = rows // 4
    for k, out in enumerate(outs):
        out[:, :128] = left[k * count : (k + 1) * count]
        out[:, 128:] = right[k * count : (k + 1) * count]


def finish_kernel(mine_ref, core_ref, far_ref, far_core_ref, coarse_ref, mid_ref, w_cout_ref, w_up_ref, out_ref):
    core = lax.axis_index("core")
    half = w_cout_ref.shape[0] // 2
    attended = jnp.zeros(coarse_ref.shape, F32)
    for heads, states in ((core, (mine_ref, far_ref)), (1 - core, (core_ref, far_core_ref))):
        _, total, acc = merged([state[...] for state in states])
        value = (acc / total).astype(BF)
        value = jnp.concatenate([value[:, 3 * HD :], value[:, : 2 * HD]], axis=1)
        attended += dot(value, w_cout_ref[pl.ds(pl.multiple_of(heads * half, half), half), :])
    coarse_mid = (coarse_ref[...].astype(F32) + attended).astype(BF)
    upper = dot(coarse_mid, w_up_ref[...])
    upper = jnp.concatenate([upper[:, part * D : (part + 1) * D] for part in range(4)], axis=0)
    fine = (mid_ref[...].astype(F32) + upper).astype(BF)
    out_ref[...] = dot(one_hot(natural_of(iota((N, N), 1)) == iota((N, N), 0)), fine).astype(BF)


def call(kernel, outs, scratch=(), smem=0, micros=0, short=False, unplaced=0):
    vmem = pl.BlockSpec(memory_space=pltpu.VMEM)
    cost = pl.CostEstimate(flops=micros * 10**9, transcendentals=0, bytes_accessed=micros << 21) if micros else None
    if short:
        cost = pl.CostEstimate(flops=1000, transcendentals=0, bytes_accessed=1000)

    def run(*args):
        return pl.pallas_call(
            kernel,
            out_shape=[jax.ShapeDtypeStruct(shape, BF if kind is None else kind) for shape, kind in outs],
            in_specs=[pl.BlockSpec(memory_space=pltpu.SMEM)] * smem + [vmem] * (len(args) - smem),
            out_specs=[vmem] * (len(outs) - unplaced) + [pl.BlockSpec(memory_space=pl.ANY)] * unplaced,
            scratch_shapes=list(scratch),
            cost_estimate=cost,
            compiler_params=pltpu.CompilerParams(vmem_limit_bytes=40 * 1024 * 1024),
        )(*args)

    return run


def permuted(value, target):
    pairs = []
    for at in itertools.product(*(range(size) for size in SIZES)):
        to = target(*at)
        if to is not None:
            pairs.append((int(np.ravel_multi_index(at, SIZES)), int(np.ravel_multi_index(to, SIZES))))
    return lax.ppermute(value, AXES, pairs)


def partner(index, far):
    other = index ^ 1 if not far else (index + 1 if index % 2 else index - 1)
    return other if 0 <= other < 16 else None


def row_partner(far):
    def target(zl, y, zh, x, core):
        to = partner(zl * 4 + y, far)
        return None if to is None else (to // 4, to % 4, zh, x, core)

    return target


def col_partner(far):
    def target(zl, y, zh, x, core):
        to = partner(zh * 8 + x * 2 + core, far)
        return None if to is None else (zl, y, to // 8, to // 2 % 4, to % 2)

    return target


def along_z(step):
    def target(zl, y, zh, x, core):
        z = (zh * 4 + zl) ^ step
        return (z % 4, y, z // 4, x, core)

    return target


def other_core(zl, y, zh, x, core):
    return (zl, y, zh, x, 1 - core)


def far_chip(zl, y, zh, x, core):
    return (zl ^ 1, y, zh, x, core)


def far_other(zl, y, zh, x, core):
    return (zl ^ 1, y, zh, x, 1 - core)


def per_device(tokens, stale_kv, timestep, w_time, w_qkv, w_out, w_merge, w_cqkv, w_cout, w_up):
    width, coarse_width = w_cout.shape
    count = N // 4
    band = ((3, SIDE, 2 * D), None)
    row_near, row_far = call(rows_kernel, [band, band], micros=4)(stale_kv)
    row_near = permuted(row_near, row_partner(False))
    row_far = permuted(row_far, row_partner(True))
    query, kv, fresh_kv, gate, mine = call(
        project_kernel,
        [((N, D), None), ((N, 2 * D), None), ((N, 2 * D), None), ((8, D), F32), ((N, D), None)],
        smem=1,
        micros=8,
    )(timestep, tokens.reshape(N, D), w_time, w_qkv)
    col_near, col_far = call(columns_kernel, [((EDGE, 2 * D), None)] * 2, micros=2)(stale_kv, row_near, row_far)
    col_near = permuted(col_near, col_partner(False))
    col_far = permuted(col_far, col_partner(True))
    mid, coarse, cq, other, ckv = call(
        fine_kernel,
        [((N, D), None), ((count, coarse_width), None), ((count, 256), None), ((count, 256), None), ((16, 2, count, width), None)],
        scratch=[pltpu.VMEM((N, 2 * D), BF), pltpu.VMEM((2, count, width), BF), pltpu.SemaphoreType.DMA((16,))],
        micros=3,
        unplaced=1,
    )(query, kv, gate, mine, row_near, row_far, col_near, col_far, w_out, w_merge, w_cqkv)
    ckv = lax.all_to_all(ckv.reshape(32, count, width), ("y", "x", "core"), 0, 0)
    other = permuted(other, other_core)
    (block,) = call(chip_kernel, [((2 * count, 256), None)])(cq, other)
    block = jnp.concatenate([block, permuted(block, along_z(1))], axis=0)
    blocks = {step: permuted(block, along_z(step)) for step in (4, 2, 6)}
    keys_values = ckv.reshape(32 * count, width)
    states = []
    before = []
    for step in (4, 2, 6, 0):
        early = before + (states[:1] if step == 0 else [])
        (state,) = call(coarse_kernel, [((4 * count, 256), None)], short=True)(keys_values, blocks.get(step, block), *early)
        before = [state]
        states.append(permuted(state, along_z(step)) if step else state)
    mine, core, far, far_core = call(pair_kernel, [((count, 256), None)] * 4)(*states)
    far, core, far_core = permuted(far, far_chip), permuted(core, other_core), permuted(far_core, far_other)
    (fine_out,) = call(finish_kernel, [((N, D), None)], micros=2)(mine, core, far, far_core, coarse, mid, w_cout, w_up)
    return (fine_out.reshape(SIDE, SIDE, D), fresh_kv.reshape(SIDE, SIDE, 2 * D))


def solution(mesh):
    fine = Mesh(mesh.devices.reshape(SIZES), AXES)
    tiled = P(("zl", "y"), ("zh", "x", "core"), None)
    return jax.shard_map(
        per_device,
        mesh=fine,
        in_specs=(tiled, tiled) + (P(),) * 8,
        out_specs=(tiled, tiled),
        check_vma=False,
    )
```
